512 devices in a mesh: row: 64 (over z, y), col: 2 (over core), rhs: 4 (over x).
Axes of the slice: x: 4, y: 8, z: 8, core: 2. Of those that a mesh axis runs over, the one named last changes fastest.
Arguments:
- factor: float32 [2, 131072, 2048], P(None, 'row', 'col'), may hold values from -0.125 to 0.125
- inverses: float32 [2, 2048, 2048], P(None, 'col'), may hold values from -0.125 to 0.125
- rhs: float32 [131072, 512], P('row', 'rhs'), may hold values from -6 to 6
Outputs:
- solution: float32 [2, 2048, 512], P(None, 'col', 'rhs')
- updated: float32 [131072, 512], P(('row', 'col'), 'rhs')
The draws below stay inside these ranges and needn't reach their ends.
All inputs are finite; a program needn't handle non-finite values.
Results may differ from the reference program's by a relative error of at most 0.000084.
Values sent between devices are 32-bit elements; how exact they have to be, the bound alone decides.
A program may use at most 128 MiB of HBM per device.

```python
import jax
import jax.numpy as jnp
from jax import lax

NB = 2048
NRHS = 512
BPD = 1
M = 131072
N_ROW = 64


def block_scale(stream_key, extent, pieces, low, high):
    def one(axis_at, parts):
        heights = jax.random.uniform(jax.random.fold_in(jax.random.fold_in(stream_key, 6), axis_at), (parts,), jnp.float32, low / len(pieces), high / len(pieces))
        return jnp.repeat(jnp.exp(heights), extent[axis_at] // parts).reshape((-1,) + (1,) * (len(extent) - axis_at - 1))

    gain = one(*pieces[0])
    for cut in pieces[1:]:
        gain = gain * one(*cut)
    return gain


def gaussian(key, dims, scale, limit, shards=(), kind=jnp.bfloat16):
    factor_of = block_scale(key, dims, shards, -0.22, 0.18) if shards else 1.0
    result = jax.random.normal(key, dims, jnp.float32) * scale * factor_of
    return jnp.minimum(jnp.maximum(result, -limit), limit).astype(kind)


def setup_inputs(seed: int = 0) -> dict:
    key_of = jax.random.split(jax.random.key(seed), 4)
    return {
        "factor": gaussian(key_of[0], (2, M, NB), NB ** -0.5, 0.125, ((1, 64), (2, 2)), jnp.float32),
        "inverses": gaussian(key_of[1], (2, NB, NB), NB ** -0.5, 0.125, ((1, 2),), jnp.float32),
        "rhs": gaussian(key_of[2], (M, NRHS), 1.0, 6.0, ((0, 64), (1, 4)), jnp.float32),
    }


def reference(factor, inverses, rhs):
    precise = lax.Precision.HIGHEST
    block_count = BPD * N_ROW

    def to_blocks(matrix):
        columns = matrix.shape[-1]
        return matrix.reshape(N_ROW, BPD, NB, columns).transpose(1, 0, 2, 3).reshape(block_count, NB, columns)

    def from_blocks(matrix):
        columns = matrix.shape[-1]
        return matrix.reshape(BPD, N_ROW, NB, columns).transpose(1, 0, 2, 3).reshape(block_count * NB, columns)

    blocks = to_blocks(rhs)
    first_column = to_blocks(factor[0])
    second_column = to_blocks(factor[1])
    block_index = jnp.arange(block_count, dtype=jnp.int32)
    first_solution = jnp.dot(inverses[0], blocks[0], precision=precise, preferred_element_type=jnp.float32)
    first_update = jnp.einsum("bij,jk->bik", first_column, first_solution, precision=precise)
    blocks = blocks - jnp.where((block_index > 0)[:, None, None], first_update, jnp.float32(0.0))
    second_solution = jnp.dot(inverses[1], blocks[1], precision=precise, preferred_element_type=jnp.float32)
    second_update = jnp.einsum("bij,jk->bik", second_column, second_solution, precision=precise)
    blocks = blocks - jnp.where((block_index > 1)[:, None, None], second_update, jnp.float32(0.0))
    return jnp.stack([first_solution, second_solution]), from_blocks(blocks)
```

```python
import functools

import jax
import jax.numpy as jnp
from jax import lax
from jax.experimental import pallas as pl
from jax.experimental.pallas import tpu as pltpu
from jax.sharding import PartitionSpec as P

MESH = pl.DeviceIdType.MESH
F32 = jnp.float32
BF16 = jnp.bfloat16
SIDE = 8
FAR_FIRST = (4, 3, 5, 2, 6, 1, 7)
HALF = 512
PIECE = 64
LANES = 128
MIB = 1 << 20


def split(value):
    high = value.astype(BF16)
    return high, (value - high.astype(F32)).astype(BF16)


def kernel(
    factor, inverses, rhs, solved_out, updated_out,
    first_low, second_low, inverse_low, stage, stage_wide, b, x0, x1, w0, w1, wide, acc, other, detour,
    stage_sem, b_sem, piece_sem, scatter_sem, along_sem, across_sem, direct_sem, direct_send,
    detour_sem, detour_send, forward_send, swap_sem, swap_send, out_sem,
):
    row = lax.axis_index("row")
    col = lax.axis_index("col")
    y = lax.rem(row, SIDE)
    z = lax.div(row, SIDE)
    sibling = {"col": 1 - col}
    is_first = row == 0
    is_second = row == 1
    is_detour = (row == SIDE) | (row == 7 * SIDE)
    pending = []

    def load(matrix, index, block, rows, buffer, slot):
        return pltpu.make_async_copy(
            matrix.at[index, pl.ds(pl.multiple_of(block * rows, rows), rows)], buffer.at[slot], stage_sem.at[slot]
        )

    def prime(matrix, index, rows, buffer):
        for slot in range(4):
            load(matrix, index, slot, rows, buffer, slot).start()

    def split_block(matrix, index, rows, buffer, target, width, block, blocks):
        slot = lax.rem(block, 4)
        load(matrix, index, block, rows, buffer, slot).wait()

        def part(k, _):
            at = pl.multiple_of(k * 16, 16)
            high, low = split(buffer[slot, pl.ds(at, 16), :])
            to = pl.ds(pl.multiple_of(block * rows + at, 16), 16)
            target[to, :width] = high
            target[to, width:] = low
            return 0

        lax.fori_loop(0, rows // 16, part, 0)

        @pl.when(block + 4 < blocks)
        def _():
            load(matrix, index, block + 4, rows, buffer, slot).start()

    def split_factor(index, target):
        def step(block, _):
            split_block(factor, index, 256, stage, target, 1024, block, 8)
            return 0
        lax.fori_loop(0, 8, step, 0)

    def split_inverse(index, begin, count):
        def step(block, _):
            split_block(inverses, index, 128, stage_wide, inverse_low, 2048, block, 8)
            return 0
        lax.fori_loop(begin, begin + count, step, 0)

    def spread(value, target, at, rows, depth):
        high, low = split(value)
        for base in (0, depth):
            target[pl.ds(pl.multiple_of(base + at, 16), rows), :LANES] = high
            target[pl.ds(pl.multiple_of(base + at, 16), rows), LANES:] = low

    def spread_all(source, target, depth):
        def step(k, _):
            at = pl.multiple_of(k * 64, 64)
            spread(source[pl.ds(at, 64), :], target, at, 64, depth)
            return 0
        lax.fori_loop(0, depth // 64, step, 0)

    def product(matrix, at, rows, weights):
        both = jnp.dot(matrix[pl.ds(pl.multiple_of(at, rows), rows), :], weights[...], preferred_element_type=F32)
        return both[:, :LANES] + both[:, LANES:]

    b_copy = pltpu.make_async_copy(rhs, b, b_sem)
    b_copy.start()

    @pl.when(is_first)
    def _():
        prime(inverses, 0, 128, stage_wide)

    @pl.when(jnp.logical_not(is_first))
    def _():
        prime(factor, 0, 256, stage)

    def at(yy, zz):
        return {"row": zz * SIDE + yy}

    barrier = pltpu.get_barrier_semaphore()
    for k in range(1, SIDE):
        pl.semaphore_signal(barrier, inc=1, device_id=at(lax.rem(y + k, SIDE), z), device_id_type=MESH)
        pl.semaphore_signal(barrier, inc=1, device_id=at(y, lax.rem(z + k, SIDE)), device_id_type=MESH)
    pl.semaphore_signal(barrier, inc=1, device_id=sibling, device_id_type=MESH)

    @pl.when(is_second)
    def _():
        for k in (1, 7):
            pl.semaphore_signal(barrier, inc=1, device_id={"row": k * SIDE}, device_id_type=MESH)

    def pass_barrier():
        @pl.when(is_detour)
        def _():
            pl.semaphore_wait(barrier, 16)

        @pl.when(jnp.logical_not(is_detour))
        def _():
            pl.semaphore_wait(barrier, 15)

    def rows_of(half, index):
        return pl.ds(pl.multiple_of(half * HALF + index * PIECE, PIECE), PIECE)

    def send(condition, buffer, rows, target, send_sem, recv_sem):
        copy = pltpu.make_async_remote_copy(
            src_ref=buffer.at[rows], dst_ref=buffer.at[rows], send_sem=send_sem, recv_sem=recv_sem,
            device_id=target, device_id_type=MESH,
        )

        @pl.when(condition)
        def _():
            copy.start()

        pending.append((condition, copy))

    def scatter(which, buffer, half, index, holds):
        owner = which
        place = index if half == 0 else index * SIDE + owner
        if place == owner or place in holds:
            return
        send(row == owner, buffer, rows_of(half, index), {"row": place},
             scatter_sem.at[which, half, index], piece_sem.at[which, half, index])

    def has_all(holds):
        return functools.reduce(jnp.logical_or, [row == q for q in holds])

    def arrive(which, buffer, half, index, holds):
        @pl.when(jnp.logical_not(has_all(holds)))
        def _():
            part = buffer.at[rows_of(half, index)]
            pltpu.make_async_copy(part, part, piece_sem.at[which, half, index]).wait()

    def relay(which, buffer, holds, wait):
        owner_y = which
        for half in range(2):
            mine, cross, cross_owner = (y, z, 0) if half == 0 else (z, y, owner_y)
            if wait:
                arrive(which, buffer, half, mine, holds)
            for k in FAR_FIRST:
                there = lax.rem(cross + k, SIDE)
                target = y + there * SIDE if half == 0 else z * SIDE + there
                skip = functools.reduce(jnp.logical_or, [target == q for q in holds])
                send((cross == cross_owner) & jnp.logical_not(skip), buffer, rows_of(half, mine), {"row": target},
                     along_sem.at[which, half, k], piece_sem.at[which, half, mine])
            for k in FAR_FIRST:
                there = lax.rem(mine + k, SIDE)
                target = z * SIDE + there if half == 0 else y + there * SIDE
                skip = functools.reduce(jnp.logical_or, [target == q for q in holds])
                send(jnp.logical_not(skip), buffer, rows_of(half, mine), {"row": target},
                     across_sem.at[which, half, k], piece_sem.at[which, half, mine])

    def collect(which, buffer, holds):
        for k in (1, 7, 2, 6, 3, 5, 4):
            arrive(which, buffer, 0, lax.rem(y + k, SIDE), holds)
            arrive(which, buffer, 1, lax.rem(z + k, SIDE), holds)

    holds0, holds1 = (0, 1), (1,)

    def direct(block):
        return pltpu.make_async_remote_copy(
            src_ref=x0.at[pl.ds(block * 256, 128)], dst_ref=x0.at[pl.ds(block * 256, 128)],
            send_sem=direct_send.at[block], recv_sem=direct_sem.at[block], device_id={"row": 1}, device_id_type=MESH)

    def aside(block, way):
        return pltpu.make_async_remote_copy(
            src_ref=x0.at[pl.ds(block * 256 + 128 + way * 64, 64)], dst_ref=detour.at[pl.ds(block * 64, 64)],
            send_sem=detour_send.at[block, way], recv_sem=detour_sem.at[block],
            device_id={"row": (SIDE, 7 * SIDE)[way]}, device_id_type=MESH)

    def forward(block, way):
        return pltpu.make_async_remote_copy(
            src_ref=detour.at[pl.ds(block * 64, 64)], dst_ref=x0.at[pl.ds(block * 256 + 128 + way * 64, 64)],
            send_sem=forward_send.at[block], recv_sem=direct_sem.at[4 + block * 2 + way],
            device_id={"row": 1}, device_id_type=MESH)

    @pl.when(is_first)
    def _():
        b_copy.wait()
        spread_all(b, wide, 2048)
        for block in range(4):
            split_inverse(0, 2 * block, 2)
            x0[pl.ds(block * 256, 256), :] = product(inverse_low, block * 256, 256, wide)
            if block == 0:
                pass_barrier()
            direct(block).start()
            for way in range(2):
                aside(block, way).start()

    @pl.when(jnp.logical_not(is_first))
    def _():
        b_copy.wait()
        split_factor(0, first_low)
        pass_barrier()

    for half in range(2):
        for index in range(SIDE):
            scatter(0, x0, half, index, holds0)

    for way in range(2):
        @pl.when(row == (SIDE, 7 * SIDE)[way])
        def _():
            for block in range(4):
                part = detour.at[pl.ds(block * 64, 64)]
                pltpu.make_async_copy(part, part, detour_sem.at[block]).wait()
                forward(block, way).start()

    def swap(block):
        rows = pl.ds(pl.multiple_of(block * 512, 512), 512)
        return rows, pltpu.make_async_remote_copy(
            src_ref=acc.at[rows], dst_ref=other.at[rows], send_sem=swap_send.at[block], recv_sem=swap_sem.at[block],
            device_id=sibling, device_id_type=MESH)

    @pl.when(is_second)
    def _():
        prime(inverses, 1, 128, stage_wide)
        split_inverse(1, 0, 8)
        for block in range(4):
            part = x0.at[pl.ds(block * 256, 128)]
            pltpu.make_async_copy(part, part, direct_sem.at[block]).wait()
            for way in range(2):
                part = x0.at[pl.ds(block * 256 + 128 + way * 64, 64)]
                pltpu.make_async_copy(part, part, direct_sem.at[4 + block * 2 + way]).wait()
        spread_all(x0, w0, 1024)
        for block in range(4):
            rows, copy = swap(block)
            acc[rows, :] = product(first_low, block * 512, 512, w0)
            copy.start()

    relay_first_done = []

    @pl.when((row > 1))
    def _():
        prime(factor, 1, 256, stage)
        split_factor(1, second_low)

    relay(0, x0, holds0, True)

    @pl.when(is_second)
    def _():
        for block in range(4):
            rows, copy = swap(block)
            copy.wait_recv()

            def step(k, _):
                at_row = pl.multiple_of(block * 512 + k * 64, 64)
                here = pl.ds(at_row, 64)
                value = b[here, :] - (acc[here, :] + other[here, :])
                b[here, :] = value
                spread(value, wide, at_row, 64, 2048)
                return 0

            lax.fori_loop(0, 8, step, 0)
        for block in range(4):
            x1[pl.ds(block * 256, 256), :] = product(inverse_low, block * 256, 256, wide)

    for half in range(2):
        for index in range(SIDE):
            scatter(1, x1, half, index, holds1)
    relay(1, x1, holds1, True)

    collect(0, x0, holds0)
    solved0 = pltpu.make_async_copy(x0, solved_out.at[0], out_sem.at[0])
    solved0.start()

    @pl.when(row > 1)
    def _():
        spread_all(x0, w0, 1024)

        def step(block, _):
            at_row = pl.multiple_of(block * 512, 512)
            acc[pl.ds(at_row, 512), :] = product(first_low, at_row, 512, w0)
            return 0
        lax.fori_loop(0, 4, step, 0)

    collect(1, x1, holds1)
    solved1 = pltpu.make_async_copy(x1, solved_out.at[1], out_sem.at[1])
    solved1.start()

    mine = pl.multiple_of(col * 1024, 1024)
    theirs = pl.multiple_of((1 - col) * 1024, 1024)

    def swap_half(block):
        source = pl.ds(pl.multiple_of(theirs + block * 512, 512), 512)
        return pltpu.make_async_remote_copy(
            src_ref=acc.at[source], dst_ref=other.at[pl.ds(block * 512, 512)], send_sem=swap_send.at[block],
            recv_sem=swap_sem.at[block], device_id=sibling, device_id_type=MESH)

    @pl.when(row > 1)
    def _():
        spread_all(x1, w1, 1024)
        for block in range(2):
            here = pl.ds(pl.multiple_of(theirs + block * 512, 512), 512)
            acc[here, :] = acc[here, :] + product(second_low, theirs + block * 512, 512, w1)
            swap_half(block).start()
        for block in range(2):
            here = pl.ds(pl.multiple_of(mine + block * 512, 512), 512)
            acc[here, :] = acc[here, :] + product(second_low, mine + block * 512, 512, w1)
        for block in range(2):
            swap_half(block).wait_recv()
            here = pl.ds(pl.multiple_of(mine + block * 512, 512), 512)
            b[here, :] = b[here, :] - (acc[here, :] + other[pl.ds(block * 512, 512), :])
        for block in range(2):
            swap_half(block).wait_send()

    updated = pltpu.make_async_copy(b.at[pl.ds(mine, 1024)], updated_out, out_sem.at[2])
    updated.start()

    for condition, copy in pending:
        @pl.when(condition)
        def _():
            copy.wait_send()

    @pl.when(is_first)
    def _():
        for block in range(4):
            direct(block).wait_send()
            for way in range(2):
                aside(block, way).wait_send()

    @pl.when(is_detour)
    def _():
        for block in range(4):
            forward(block, 0).wait_send()

    @pl.when(is_second)
    def _():
        for block in range(4):
            swap(block)[1].wait_send()

    solved0.wait()
    solved1.wait()
    updated.wait()


def body(factor, inverses, rhs):
    dma = pltpu.SemaphoreType.DMA
    return pl.pallas_call(
        kernel,
        out_shape=(jax.ShapeDtypeStruct((2, 1024, LANES), F32), jax.ShapeDtypeStruct((1024, LANES), F32)),
        in_specs=[pl.BlockSpec(memory_space=pl.ANY)] * 3,
        out_specs=(pl.BlockSpec(memory_space=pl.ANY), pl.BlockSpec(memory_space=pl.ANY)),
        scratch_shapes=[
            pltpu.VMEM((2048, 2048), BF16),
            pltpu.VMEM((2048, 2048), BF16),
            pltpu.VMEM((1024, 4096), BF16),
            pltpu.VMEM((4, 256, 1024), F32),
            pltpu.VMEM((4, 128, 2048), F32),
            pltpu.VMEM((2048, LANES), F32),
            pltpu.VMEM((1024, LANES), F32),
            pltpu.VMEM((1024, LANES), F32),
            pltpu.VMEM((2048, 2 * LANES), BF16),
            pltpu.VMEM((2048, 2 * LANES), BF16),
            pltpu.VMEM((4096, 2 * LANES), BF16),
            pltpu.VMEM((2048, LANES), F32),
            pltpu.VMEM((2048, LANES), F32),
            pltpu.VMEM((256, LANES), F32),
            dma((4,)), dma, dma((2, 2, SIDE)), dma((2, 2, SIDE)), dma((2, 2, SIDE)), dma((2, 2, SIDE)),
            dma((12,)), dma((4,)), dma((4,)), dma((4, 2)), dma((4,)), dma((4,)), dma((4,)), dma((3,)),
        ],
        compiler_params=pltpu.CompilerParams(collective_id=0, has_side_effects=True, vmem_limit_bytes=56 * MIB),
        cost_estimate=pl.CostEstimate(flops=2 * 2 * 2048 * 1024 * 128, bytes_accessed=18 * MIB, transcendentals=0),
        name="block_steps",
    )(factor, inverses, rhs)


def solution(mesh):
    in_specs = (P(None, "row", "col"), P(None, "col", None), P("row", "rhs"))
    out_specs = (P(None, "col", "rhs"), P(("row", "col"), "rhs"))
    return jax.shard_map(body, mesh=mesh, in_specs=in_specs, out_specs=out_specs, check_vma=False)
```

```python
import functools

import jax
import jax.numpy as jnp
from jax import lax
from jax.experimental import pallas as pl
from jax.experimental.pallas import tpu as pltpu
from jax.sharding import PartitionSpec as P

MESH = pl.DeviceIdType.MESH
F32 = jnp.float32
BF16 = jnp.bfloat16
SIDE = 8
FAR_FIRST = (4, 3, 5, 2, 6, 1, 7)
HALF = 512
CHUNK = 256
LANES = 128
MIB = 1 << 20


def split(value):
    high = value.astype(BF16)
    return high, (value - high.astype(F32)).astype(BF16)


def kernel(
    factor, inverses, rhs, solved_out, updated_out,
    first_low, second_low, inverse_low, stage, stage_wide, b, x0, x1, w0, w1, wide, acc, other, detour,
    stage_sem, b_sem, piece_sem, scatter_sem, along_sem, across_sem, direct_sem, direct_send,
    detour_sem, detour_send, forward_send, swap_sem, swap_send, out_sem,
):
    row = lax.axis_index("row")
    col = lax.axis_index("col")
    y = lax.rem(row, SIDE)
    z = lax.div(row, SIDE)
    sibling = {"col": 1 - col}
    is_first = row == 0
    is_second = row == 1
    is_detour = (row == SIDE) | (row == 7 * SIDE)
    pending = []

    def load_factor(block):
        slot = lax.rem(block, 4)
        rows = pl.ds(pl.multiple_of(lax.rem(block, 8) * 256, 256), 256)
        return pltpu.make_async_copy(factor.at[lax.div(block, 8), rows], stage.at[slot], stage_sem.at[slot])

    def load_inverse(index, block):
        slot = lax.rem(block, 4)
        rows = pl.ds(pl.multiple_of(block * 128, 128), 128)
        return pltpu.make_async_copy(inverses.at[index, rows], stage_wide.at[slot], stage_sem.at[4 + slot])

    def split_rows(source, slot, rows, step_rows, target, base):
        chunks = source.shape[2] // CHUNK

        def part(k, _):
            at = pl.multiple_of(k * step_rows, step_rows)
            to = pl.ds(pl.multiple_of(base + at, step_rows), step_rows)
            for q in range(chunks):
                high, low = split(source[slot, pl.ds(at, step_rows), q * CHUNK:(q + 1) * CHUNK])
                target[to, 2 * q * CHUNK:(2 * q + 1) * CHUNK] = high
                target[to, (2 * q + 1) * CHUNK:(2 * q + 2) * CHUNK] = low
            return 0

        lax.fori_loop(0, rows // step_rows, part, 0)

    def split_factor(index, target, blocks):
        def step(k, _):
            block = index * 8 + k
            load_factor(block).wait()
            split_rows(stage, lax.rem(block, 4), 256, 64, target, k * 256)

            @pl.when(block + 4 < blocks)
            def _():
                load_factor(block + 4).start()
            return 0
        lax.fori_loop(0, 8, step, 0)

    def split_inverse(index, begin, count):
        def step(block, _):
            load_inverse(index, block).wait()
            split_rows(stage_wide, lax.rem(block, 4), 128, 32, inverse_low, block * 128)

            @pl.when(block + 4 < 8)
            def _():
                load_inverse(index, block + 4).start()
            return 0
        lax.fori_loop(begin, begin + count, step, 0)

    def spread(value, target, at):
        rows = value.shape[0]
        high, low = split(value)
        chunk, inside = lax.div(at, CHUNK), lax.rem(at, CHUNK)
        for part in range(2):
            to = pl.ds(pl.multiple_of(chunk * 2 * CHUNK + part * CHUNK + inside, 64), rows)
            target[to, :LANES] = high
            target[to, LANES:] = low

    def spread_rows(source, target, begin, count):
        def step(k, _):
            at = pl.multiple_of(begin + k * CHUNK, CHUNK)
            spread(source[pl.ds(at, CHUNK), :], target, at)
            return 0
        lax.fori_loop(0, count // CHUNK, step, 0)

    def product(matrix, at, rows, weights, first, count):
        columns = slice(2 * first * CHUNK, 2 * (first + count) * CHUNK)
        both = jnp.dot(matrix[pl.ds(pl.multiple_of(at, rows), rows), columns], weights[columns, :],
                       preferred_element_type=F32)
        return both[:, :LANES] + both[:, LANES:]

    b_copy = pltpu.make_async_copy(rhs, b, b_sem)
    b_copy.start()

    @pl.when(is_first | is_second)
    def _():
        for block in range(4):
            load_inverse(row, jnp.int32(block)).start()

    @pl.when(jnp.logical_not(is_first))
    def _():
        for block in range(4):
            load_factor(jnp.int32(block)).start()

    def at(yy, zz):
        return {"row": zz * SIDE + yy}

    barrier = pltpu.get_barrier_semaphore()
    for k in range(1, SIDE):
        pl.semaphore_signal(barrier, inc=1, device_id=at(lax.rem(y + k, SIDE), z), device_id_type=MESH)
        pl.semaphore_signal(barrier, inc=1, device_id=at(y, lax.rem(z + k, SIDE)), device_id_type=MESH)
    pl.semaphore_signal(barrier, inc=1, device_id=sibling, device_id_type=MESH)

    @pl.when(is_second)
    def _():
        for k in (1, 7):
            pl.semaphore_signal(barrier, inc=1, device_id={"row": k * SIDE}, device_id_type=MESH)

    def pass_barrier():
        @pl.when(is_detour)
        def _():
            pl.semaphore_wait(barrier, 16)

        @pl.when(jnp.logical_not(is_detour))
        def _():
            pl.semaphore_wait(barrier, 15)

    def layout(which, half):
        if which == 0 and half == 0:
            return 80, 32, 0, (0, 1)
        return 72, 8, (which if half == 0 else 0), ((which,) if half == 0 else (0,))

    def hub_rows(which, half, index):
        rows, _, owner, outside = layout(which, half)
        rank = index - len(outside) if owner == 0 else index - jnp.where(index > owner, 1, 0)
        return pl.ds(pl.multiple_of(half * HALF + rank * rows, 8), rows)

    def rest_rows(which, half):
        rest = layout(which, half)[1]
        return pl.ds((half + 1) * HALF - rest, rest)

    def is_hub(which, half, index):
        return functools.reduce(jnp.logical_and, [index != q for q in layout(which, half)[3]])

    def send(condition, buffer, rows, target, send_sem, recv_sem):
        copy = pltpu.make_async_remote_copy(
            src_ref=buffer.at[rows], dst_ref=buffer.at[rows], send_sem=send_sem, recv_sem=recv_sem,
            device_id=target, device_id_type=MESH,
        )

        @pl.when(condition)
        def _():
            copy.start()

        pending.append((condition, copy))

    def scatter(which, buffer, half, index):
        owner = which
        if index in layout(which, half)[3]:
            return
        place = index if half == 0 else index * SIDE + owner
        send(row == owner, buffer, hub_rows(which, half, jnp.int32(index)), {"row": place},
             scatter_sem.at[which, half, index], piece_sem.at[which, half, index])

    def among(place, holds):
        return functools.reduce(jnp.logical_or, [place == q for q in holds])

    def arrive(which, buffer, half, index, holds):
        outside = among(row, holds)

        def wait(rows):
            part = buffer.at[rows]
            pltpu.make_async_copy(part, part, piece_sem.at[which, half, index]).wait()

        @pl.when(jnp.logical_not(outside) & is_hub(which, half, index))
        def _():
            wait(hub_rows(which, half, index))

        @pl.when(jnp.logical_not(outside) & (index == layout(which, half)[2]))
        def _():
            wait(rest_rows(which, half))

    def relay(which, buffer, holds):
        for half in range(2):
            mine, cross, cross_owner = (y, z, 0) if half == 0 else (z, y, which)
            arrive(which, buffer, half, mine, holds)
            for step, sems in ((0, along_sem), (1, across_sem)):
                for k in FAR_FIRST:
                    if step == 0:
                        there = lax.rem(cross + k, SIDE)
                        target = y + there * SIDE if half == 0 else z * SIDE + there
                    else:
                        there = lax.rem(mine + k, SIDE)
                        target = z * SIDE + there if half == 0 else y + there * SIDE
                    go = jnp.logical_not(among(target, holds))
                    if step == 0:
                        go = go & (cross == cross_owner)
                    send(go & is_hub(which, half, mine), buffer, hub_rows(which, half, mine), {"row": target},
                         sems.at[which, half, k], piece_sem.at[which, half, mine])
                    send(go & (mine == layout(which, half)[2]), buffer, rest_rows(which, half), {"row": target},
                         sems.at[which, half, k], piece_sem.at[which, half, mine])

    def collect(which, buffer, half, holds):
        for k in (1, 7, 2, 6, 3, 5, 4):
            arrive(which, buffer, half, lax.rem((y if half == 0 else z) + k, SIDE), holds)

    holds0, holds1 = (0, 1), (1,)

    def direct(block):
        return pltpu.make_async_remote_copy(
            src_ref=x0.at[pl.ds(block * 256, 128)], dst_ref=x0.at[pl.ds(block * 256, 128)],
            send_sem=direct_send.at[block], recv_sem=direct_sem.at[block], device_id={"row": 1}, device_id_type=MESH)

    def aside(block, way):
        return pltpu.make_async_remote_copy(
            src_ref=x0.at[pl.ds(block * 256 + 128 + way * 64, 64)], dst_ref=detour.at[pl.ds(block * 64, 64)],
            send_sem=detour_send.at[block, way], recv_sem=detour_sem.at[block],
            device_id={"row": (SIDE, 7 * SIDE)[way]}, device_id_type=MESH)

    def forward(block, way):
        return pltpu.make_async_remote_copy(
            src_ref=detour.at[pl.ds(block * 64, 64)], dst_ref=x0.at[pl.ds(block * 256 + 128 + way * 64, 64)],
            send_sem=forward_send.at[block], recv_sem=direct_sem.at[4 + block * 2 + way],
            device_id={"row": 1}, device_id_type=MESH)

    @pl.when(is_first)
    def _():
        b_copy.wait()
        spread_rows(b, wide, 0, 2048)
        for block in range(4):
            split_inverse(0, 2 * block, 2)
            x0[pl.ds(block * 256, 256), :] = product(inverse_low, block * 256, 256, wide, 0, 8)
            if block == 0:
                pass_barrier()
            direct(block).start()
            for way in range(2):
                aside(block, way).start()

    @pl.when(jnp.logical_not(is_first))
    def _():
        b_copy.wait()
        split_factor(0, first_low, jnp.where(is_second, 8, 16))
        pass_barrier()

    for index in (5, 6, 7):
        scatter(0, x0, 0, index)
    for index in (4, 3, 5, 2, 6, 1, 7):
        scatter(0, x0, 1, index)
    for index in (4, 3, 2):
        scatter(0, x0, 0, index)

    for way in range(2):
        @pl.when(row == (SIDE, 7 * SIDE)[way])
        def _():
            for block in range(4):
                part = detour.at[pl.ds(block * 64, 64)]
                pltpu.make_async_copy(part, part, detour_sem.at[block]).wait()
                forward(block, way).start()

    def swap(block):
        rows = pl.ds(pl.multiple_of(block * 512, 512), 512)
        return rows, pltpu.make_async_remote_copy(
            src_ref=acc.at[rows], dst_ref=other.at[rows], send_sem=swap_send.at[block], recv_sem=swap_sem.at[block],
            device_id=sibling, device_id_type=MESH)

    @pl.when(is_second)
    def _():
        split_inverse(1, 0, 8)
        for chunk in range(4):
            part = x0.at[pl.ds(chunk * 256, 128)]
            pltpu.make_async_copy(part, part, direct_sem.at[chunk]).wait()
            for way in range(2):
                part = x0.at[pl.ds(chunk * 256 + 128 + way * 64, 64)]
                pltpu.make_async_copy(part, part, direct_sem.at[4 + chunk * 2 + way]).wait()
            spread_rows(x0, w0, chunk * CHUNK, CHUNK)
            for block in range(4):
                rows, copy = swap(block)
                term = product(first_low, block * 512, 512, w0, chunk, 1)
                acc[rows, :] = term if chunk == 0 else acc[rows, :] + term
                if chunk == 3:
                    copy.start()

    @pl.when(row > 1)
    def _():
        split_factor(1, second_low, 16)

    relay(0, x0, holds0)

    @pl.when(is_second)
    def _():
        for block in range(4):
            rows, copy = swap(block)
            copy.wait_recv()
            for part in range(2):
                here = pl.ds(block * 512 + part * CHUNK, CHUNK)
                value = b[here, :] - (acc[here, :] + other[here, :])
                b[here, :] = value
                spread(value, wide, jnp.int32(block * 512 + part * CHUNK))
            for part in range(2):
                here = pl.ds(part * 512, 512)
                term = product(inverse_low, part * 512, 512, wide, 2 * block, 2)
                x1[here, :] = term if block == 0 else x1[here, :] + term

    for index in (5, 4, 6, 3, 7, 0, 2):
        scatter(1, x1, 0, index)
        scatter(1, x1, 1, (index + 7) % SIDE)
    relay(1, x1, holds1)

    collect(0, x0, 0, holds0)
    collect(0, x0, 1, holds0)
    solved0 = pltpu.make_async_copy(x0, solved_out.at[0], out_sem.at[0])
    solved0.start()

    @pl.when(row > 1)
    def _():
        spread_rows(x0, w0, 0, 1024)

        def step(block, _):
            at_row = pl.multiple_of(block * 512, 512)
            acc[pl.ds(at_row, 512), :] = product(first_low, at_row, 512, w0, 0, 4)
            return 0
        lax.fori_loop(0, 4, step, 0)

    collect(1, x1, 0, holds1)

    @pl.when(row > 1)
    def _():
        spread_rows(x1, w1, 0, 512)

        def step(block, _):
            at_row = pl.multiple_of(block * 512, 512)
            rows = pl.ds(at_row, 512)
            acc[rows, :] = acc[rows, :] + product(second_low, at_row, 512, w1, 0, 2)
            return 0
        lax.fori_loop(0, 4, step, 0)

    collect(1, x1, 1, holds1)
    solved1 = pltpu.make_async_copy(x1, solved_out.at[1], out_sem.at[1])
    solved1.start()

    mine = pl.multiple_of(col * 1024, 1024)
    theirs = pl.multiple_of((1 - col) * 1024, 1024)

    def swap_half(block):
        source = pl.ds(pl.multiple_of(theirs + block * 512, 512), 512)
        return pltpu.make_async_remote_copy(
            src_ref=acc.at[source], dst_ref=other.at[pl.ds(block * 512, 512)], send_sem=swap_send.at[block],
            recv_sem=swap_sem.at[block], device_id=sibling, device_id_type=MESH)

    @pl.when(row > 1)
    def _():
        spread_rows(x1, w1, 512, 512)
        for block in range(2):
            here = pl.ds(pl.multiple_of(theirs + block * 512, 512), 512)
            acc[here, :] = acc[here, :] + product(second_low, theirs + block * 512, 512, w1, 2, 2)
            swap_half(block).start()
        for block in range(2):
            here = pl.ds(pl.multiple_of(mine + block * 512, 512), 512)
            b[here, :] = b[here, :] - (acc[here, :] + product(second_low, mine + block * 512, 512, w1, 2, 2))
        for block in range(2):
            swap_half(block).wait_recv()
            here = pl.ds(pl.multiple_of(mine + block * 512, 512), 512)
            b[here, :] = b[here, :] - other[pl.ds(block * 512, 512), :]
        for block in range(2):
            swap_half(block).wait_send()

    updated = pltpu.make_async_copy(b.at[pl.ds(mine, 1024)], updated_out, out_sem.at[2])
    updated.start()

    for condition, copy in pending:
        @pl.when(condition)
        def _():
            copy.wait_send()

    @pl.when(is_first)
    def _():
        for block in range(4):
            direct(block).wait_send()
            for way in range(2):
                aside(block, way).wait_send()

    @pl.when(is_detour)
    def _():
        for block in range(4):
            forward(block, 0).wait_send()

    @pl.when(is_second)
    def _():
        for block in range(4):
            swap(block)[1].wait_send()

    solved0.wait()
    solved1.wait()
    updated.wait()


def body(factor, inverses, rhs):
    dma = pltpu.SemaphoreType.DMA
    return pl.pallas_call(
        kernel,
        out_shape=(jax.ShapeDtypeStruct((2, 1024, LANES), F32), jax.ShapeDtypeStruct((1024, LANES), F32)),
        in_specs=[pl.BlockSpec(memory_space=pl.ANY)] * 3,
        out_specs=(pl.BlockSpec(memory_space=pl.ANY), pl.BlockSpec(memory_space=pl.ANY)),
        scratch_shapes=[
            pltpu.VMEM((2048, 2048), BF16),
            pltpu.VMEM((2048, 2048), BF16),
            pltpu.VMEM((1024, 4096), BF16),
            pltpu.VMEM((4, 256, 1024), F32),
            pltpu.VMEM((4, 128, 2048), F32),
            pltpu.VMEM((2048, LANES), F32),
            pltpu.VMEM((1024, LANES), F32),
            pltpu.VMEM((1024, LANES), F32),
            pltpu.VMEM((2048, 2 * LANES), BF16),
            pltpu.VMEM((2048, 2 * LANES), BF16),
            pltpu.VMEM((4096, 2 * LANES), BF16),
            pltpu.VMEM((2048, LANES), F32),
            pltpu.VMEM((2048, LANES), F32),
            pltpu.VMEM((256, LANES), F32),
            dma((8,)), dma, dma((2, 2, SIDE)), dma((2, 2, SIDE)), dma((2, 2, SIDE)), dma((2, 2, SIDE)),
            dma((12,)), dma((4,)), dma((4,)), dma((4, 2)), dma((4,)), dma((4,)), dma((4,)), dma((3,)),
        ],
        compiler_params=pltpu.CompilerParams(collective_id=0, has_side_effects=True, vmem_limit_bytes=56 * MIB),
        cost_estimate=pl.CostEstimate(flops=2 * 2 * 2048 * 1024 * 128, bytes_accessed=18 * MIB, transcendentals=0),
        name="block_steps",
    )(factor, inverses, rhs)


def solution(mesh):
    in_specs = (P(None, "row", "col"), P(None, "col", None), P("row", "rhs"))
    out_specs = (P(None, "col", "rhs"), P(("row", "col"), "rhs"))
    return jax.shard_map(body, mesh=mesh, in_specs=in_specs, out_specs=out_specs, check_vma=False)
```

```python
import functools

import jax
import jax.numpy as jnp
from jax import lax
from jax.experimental import pallas as pl
from jax.experimental.pallas import tpu as pltpu
from jax.sharding import PartitionSpec as P

MESH = pl.DeviceIdType.MESH
F32 = jnp.float32
BF16 = jnp.bfloat16
SIDE = 8
FAR_FIRST = (4, 3, 5, 2, 6, 1, 7)
HALF = 512
CHUNK = 256
LANES = 128
MIB = 1 << 20


def split(value):
    high = value.astype(BF16)
    return high, (value - high.astype(F32)).astype(BF16)


def kernel(
    factor, inverses, rhs, solved_out, updated_out,
    first_low, second_low, inverse_low, stage, stage_wide, b, x0, x1, w0, w1, wide, acc, other, detour,
    stage_sem, b_sem, piece_sem, scatter_sem, along_sem, across_sem, direct_sem, direct_send,
    detour_sem, detour_send, forward_send, swap_sem, swap_send, out_sem,
):
    row = lax.axis_index("row")
    col = lax.axis_index("col")
    y = lax.rem(row, SIDE)
    z = lax.div(row, SIDE)
    sibling = {"col": 1 - col}
    is_first = row == 0
    is_second = row == 1
    is_detour = (row == SIDE) | (row == 7 * SIDE)
    pending = []

    def load_factor(block):
        slot = lax.rem(block, 4)
        rows = pl.ds(pl.multiple_of(lax.rem(block, 8) * 256, 256), 256)
        return pltpu.make_async_copy(factor.at[lax.div(block, 8), rows], stage.at[slot], stage_sem.at[slot])

    def load_inverse(index, block):
        rows = pl.ds(pl.multiple_of(block * 256, 256), 256)
        return pltpu.make_async_copy(inverses.at[index, rows], stage_wide.at[block], stage_sem.at[4 + block])

    def split_rows(source, slot, rows, step_rows, target, base):
        chunks = source.shape[2] // CHUNK

        def part(k, _):
            at = pl.multiple_of(k * step_rows, step_rows)
            to = pl.ds(pl.multiple_of(base + at, step_rows), step_rows)
            for q in range(chunks):
                high, low = split(source[slot, pl.ds(at, step_rows), q * CHUNK:(q + 1) * CHUNK])
                target[to, 2 * q * CHUNK:(2 * q + 1) * CHUNK] = high
                target[to, (2 * q + 1) * CHUNK:(2 * q + 2) * CHUNK] = low
            return 0

        lax.fori_loop(0, rows // step_rows, part, 0)

    def split_factor(index, target, blocks):
        def step(k, _):
            block = index * 8 + k
            load_factor(block).wait()
            split_rows(stage, lax.rem(block, 4), 256, 64, target, k * 256)

            @pl.when(block + 4 < blocks)
            def _():
                load_factor(block + 4).start()
            return 0
        lax.fori_loop(0, 8, step, 0)

    def split_inverse(index):
        def step(block, _):
            load_inverse(index, block).wait()
            split_rows(stage_wide, block, 256, 32, inverse_low, block * 256)
            return 0
        lax.fori_loop(0, 4, step, 0)

    def spread(value, target, at):
        rows = value.shape[0]
        high, low = split(value)
        chunk, inside = lax.div(at, CHUNK), lax.rem(at, CHUNK)
        for part in range(2):
            to = pl.ds(pl.multiple_of(chunk * 2 * CHUNK + part * CHUNK + inside, 64), rows)
            target[to, :LANES] = high
            target[to, LANES:] = low

    def spread_rows(source, target, begin, count):
        def step(k, _):
            at = pl.multiple_of(begin + k * CHUNK, CHUNK)
            spread(source[pl.ds(at, CHUNK), :], target, at)
            return 0
        lax.fori_loop(0, count // CHUNK, step, 0)

    def product(matrix, at, rows, weights, first, count):
        columns = slice(2 * first * CHUNK, 2 * (first + count) * CHUNK)
        both = jnp.dot(matrix[pl.ds(pl.multiple_of(at, rows), rows), columns], weights[columns, :],
                       preferred_element_type=F32)
        return both[:, :LANES] + both[:, LANES:]

    def split_product(source, slot, weights):
        total = None
        for q in range(source.shape[2] // CHUNK):
            parts = jnp.concatenate(split(source[slot, :, q * CHUNK:(q + 1) * CHUNK]), axis=0)
            term = jnp.dot(parts, weights[2 * q * CHUNK:(2 * q + 1) * CHUNK, :], preferred_element_type=F32)
            total = term if total is None else total + term
        both = total[:256, :] + total[256:, :]
        return both[:, :LANES] + both[:, LANES:]

    b_copy = pltpu.make_async_copy(rhs, b, b_sem)
    b_copy.start()

    @pl.when(is_first | is_second)
    def _():
        for block in range(4):
            load_inverse(row, jnp.int32(block)).start()

    @pl.when(jnp.logical_not(is_first))
    def _():
        for block in range(4):
            load_factor(jnp.int32(block)).start()

    def at(yy, zz):
        return {"row": zz * SIDE + yy}

    barrier = pltpu.get_barrier_semaphore()
    for k in range(1, SIDE):
        pl.semaphore_signal(barrier, inc=1, device_id=at(lax.rem(y + k, SIDE), z), device_id_type=MESH)
        pl.semaphore_signal(barrier, inc=1, device_id=at(y, lax.rem(z + k, SIDE)), device_id_type=MESH)
    pl.semaphore_signal(barrier, inc=1, device_id=sibling, device_id_type=MESH)

    @pl.when(is_second)
    def _():
        for k in (1, 7):
            pl.semaphore_signal(barrier, inc=1, device_id={"row": k * SIDE}, device_id_type=MESH)

    def pass_barrier():
        @pl.when(is_detour)
        def _():
            pl.semaphore_wait(barrier, 16)

        @pl.when(jnp.logical_not(is_detour))
        def _():
            pl.semaphore_wait(barrier, 15)

    def layout(which, half):
        if which == 0 and half == 0:
            return 80, 32, 0, (0, 1)
        return 72, 8, (which if half == 0 else 0), ((which,) if half == 0 else (0,))

    def hub_rows(which, half, index):
        rows, _, owner, outside = layout(which, half)
        rank = index - len(outside) if owner == 0 else index - jnp.where(index > owner, 1, 0)
        return pl.ds(pl.multiple_of(half * HALF + rank * rows, 8), rows)

    def rest_rows(which, half):
        rest = layout(which, half)[1]
        return pl.ds((half + 1) * HALF - rest, rest)

    def is_hub(which, half, index):
        return functools.reduce(jnp.logical_and, [index != q for q in layout(which, half)[3]])

    def send(condition, buffer, rows, target, send_sem, recv_sem):
        copy = pltpu.make_async_remote_copy(
            src_ref=buffer.at[rows], dst_ref=buffer.at[rows], send_sem=send_sem, recv_sem=recv_sem,
            device_id=target, device_id_type=MESH,
        )

        @pl.when(condition)
        def _():
            copy.start()

        pending.append((condition, copy))

    def scatter(which, buffer, half, index):
        owner = which
        if index in layout(which, half)[3]:
            return
        place = index if half == 0 else index * SIDE + owner
        send(row == owner, buffer, hub_rows(which, half, jnp.int32(index)), {"row": place},
             scatter_sem.at[which, half, index], piece_sem.at[which, half, index])

    def among(place, holds):
        return functools.reduce(jnp.logical_or, [place == q for q in holds])

    def arrive(which, buffer, half, index, holds):
        outside = among(row, holds)

        def wait(rows):
            part = buffer.at[rows]
            pltpu.make_async_copy(part, part, piece_sem.at[which, half, index]).wait()

        @pl.when(jnp.logical_not(outside) & is_hub(which, half, index))
        def _():
            wait(hub_rows(which, half, index))

        @pl.when(jnp.logical_not(outside) & (index == layout(which, half)[2]))
        def _():
            wait(rest_rows(which, half))

    def relay(which, buffer, holds):
        for half in range(2):
            mine, cross, cross_owner = (y, z, 0) if half == 0 else (z, y, which)
            arrive(which, buffer, half, mine, holds)
            for step, sems in ((0, along_sem), (1, across_sem)):
                for k in FAR_FIRST:
                    if step == 0:
                        there = lax.rem(cross + k, SIDE)
                        target = y + there * SIDE if half == 0 else z * SIDE + there
                    else:
                        there = lax.rem(mine + k, SIDE)
                        target = z * SIDE + there if half == 0 else y + there * SIDE
                    go = jnp.logical_not(among(target, holds))
                    if step == 0:
                        go = go & (cross == cross_owner)
                    send(go & is_hub(which, half, mine), buffer, hub_rows(which, half, mine), {"row": target},
                         sems.at[which, half, k], piece_sem.at[which, half, mine])
                    send(go & (mine == layout(which, half)[2]), buffer, rest_rows(which, half), {"row": target},
                         sems.at[which, half, k], piece_sem.at[which, half, mine])

    def collect(which, buffer, half, holds):
        for k in (1, 7, 2, 6, 3, 5, 4):
            arrive(which, buffer, half, lax.rem((y if half == 0 else z) + k, SIDE), holds)

    holds0, holds1 = (0, 1), (1,)

    def direct(block):
        return pltpu.make_async_remote_copy(
            src_ref=x0.at[pl.ds(block * 256, 128)], dst_ref=x0.at[pl.ds(block * 256, 128)],
            send_sem=direct_send.at[block], recv_sem=direct_sem.at[block], device_id={"row": 1}, device_id_type=MESH)

    def aside(block, way):
        return pltpu.make_async_remote_copy(
            src_ref=x0.at[pl.ds(block * 256 + 128 + way * 64, 64)], dst_ref=detour.at[pl.ds(block * 64, 64)],
            send_sem=detour_send.at[block, way], recv_sem=detour_sem.at[block],
            device_id={"row": (SIDE, 7 * SIDE)[way]}, device_id_type=MESH)

    def forward(block, way):
        return pltpu.make_async_remote_copy(
            src_ref=detour.at[pl.ds(block * 64, 64)], dst_ref=x0.at[pl.ds(block * 256 + 128 + way * 64, 64)],
            send_sem=forward_send.at[block], recv_sem=direct_sem.at[4 + block * 2 + way],
            device_id={"row": 1}, device_id_type=MESH)

    @pl.when(is_first)
    def _():
        b_copy.wait()
        spread_rows(b, wide, 0, 2048)
        for block in range(4):
            load_inverse(0, jnp.int32(block)).wait()
            x0[pl.ds(block * 256, 256), :] = split_product(stage_wide, block, wide)
            if block == 0:
                pass_barrier()
            direct(block).start()
            for way in range(2):
                aside(block, way).start()

    @pl.when(jnp.logical_not(is_first))
    def _():
        b_copy.wait()
        split_factor(0, first_low, jnp.where(is_second, 8, 16))
        pass_barrier()

    for index in (5, 6, 7):
        scatter(0, x0, 0, index)
    for index in (4, 3, 5, 2, 6, 1, 7):
        scatter(0, x0, 1, index)
    for index in (4, 3, 2):
        scatter(0, x0, 0, index)

    for way in range(2):
        @pl.when(row == (SIDE, 7 * SIDE)[way])
        def _():
            for block in range(4):
                part = detour.at[pl.ds(block * 64, 64)]
                pltpu.make_async_copy(part, part, detour_sem.at[block]).wait()
                forward(block, way).start()

    def swap(block):
        rows = pl.ds(pl.multiple_of(block * 512, 512), 512)
        return rows, pltpu.make_async_remote_copy(
            src_ref=acc.at[rows], dst_ref=other.at[rows], send_sem=swap_send.at[block], recv_sem=swap_sem.at[block],
            device_id=sibling, device_id_type=MESH)

    @pl.when(is_second)
    def _():
        split_inverse(1)
        for chunk in range(4):
            part = x0.at[pl.ds(chunk * 256, 128)]
            pltpu.make_async_copy(part, part, direct_sem.at[chunk]).wait()
            for way in range(2):
                part = x0.at[pl.ds(chunk * 256 + 128 + way * 64, 64)]
                pltpu.make_async_copy(part, part, direct_sem.at[4 + chunk * 2 + way]).wait()
            spread_rows(x0, w0, chunk * CHUNK, CHUNK)
            for block in range(4):
                rows, copy = swap(block)
                term = product(first_low, block * 512, 512, w0, chunk, 1)
                acc[rows, :] = term if chunk == 0 else acc[rows, :] + term
                if chunk == 3:
                    copy.start()

    @pl.when(row > 1)
    def _():
        split_factor(1, second_low, 16)

    relay(0, x0, holds0)

    @pl.when(is_second)
    def _():
        for block in range(4):
            rows, copy = swap(block)
            copy.wait_recv()
            for part in range(2):
                here = pl.ds(block * 512 + part * CHUNK, CHUNK)
                value = b[here, :] - (acc[here, :] + other[here, :])
                b[here, :] = value
                spread(value, wide, jnp.int32(block * 512 + part * CHUNK))
            for part in range(2):
                here = pl.ds(part * 512, 512)
                term = product(inverse_low, part * 512, 512, wide, 2 * block, 2)
                x1[here, :] = term if block == 0 else x1[here, :] + term

    for index in (5, 4, 6, 3, 7, 0, 2):
        scatter(1, x1, 0, index)
        scatter(1, x1, 1, (index + 7) % SIDE)
    relay(1, x1, holds1)

    collect(0, x0, 0, holds0)
    collect(0, x0, 1, holds0)
    solved0 = pltpu.make_async_copy(x0, solved_out.at[0], out_sem.at[0])
    solved0.start()

    @pl.when(row > 1)
    def _():
        spread_rows(x0, w0, 0, 1024)

        def step(block, _):
            at_row = pl.multiple_of(block * 512, 512)
            acc[pl.ds(at_row, 512), :] = product(first_low, at_row, 512, w0, 0, 4)
            return 0
        lax.fori_loop(0, 4, step, 0)

    collect(1, x1, 0, holds1)

    @pl.when(row > 1)
    def _():
        spread_rows(x1, w1, 0, 512)

        def step(block, _):
            at_row = pl.multiple_of(block * 512, 512)
            rows = pl.ds(at_row, 512)
            acc[rows, :] = acc[rows, :] + product(second_low, at_row, 512, w1, 0, 2)
            return 0
        lax.fori_loop(0, 4, step, 0)

    collect(1, x1, 1, holds1)
    solved1 = pltpu.make_async_copy(x1, solved_out.at[1], out_sem.at[1])
    solved1.start()

    mine = pl.multiple_of(col * 1024, 1024)
    theirs = pl.multiple_of((1 - col) * 1024, 1024)

    def swap_half(block):
        source = pl.ds(pl.multiple_of(theirs + block * 512, 512), 512)
        return pltpu.make_async_remote_copy(
            src_ref=acc.at[source], dst_ref=other.at[pl.ds(block * 512, 512)], send_sem=swap_send.at[block],
            recv_sem=swap_sem.at[block], device_id=sibling, device_id_type=MESH)

    @pl.when(row > 1)
    def _():
        spread_rows(x1, w1, 512, 512)
        for block in range(2):
            here = pl.ds(pl.multiple_of(theirs + block * 512, 512), 512)
            acc[here, :] = acc[here, :] + product(second_low, theirs + block * 512, 512, w1, 2, 2)
            swap_half(block).start()
        for block in range(2):
            here = pl.ds(pl.multiple_of(mine + block * 512, 512), 512)
            b[here, :] = b[here, :] - (acc[here, :] + product(second_low, mine + block * 512, 512, w1, 2, 2))
        for block in range(2):
            swap_half(block).wait_recv()
            here = pl.ds(pl.multiple_of(mine + block * 512, 512), 512)
            b[here, :] = b[here, :] - other[pl.ds(block * 512, 512), :]
        for block in range(2):
            swap_half(block).wait_send()

    updated = pltpu.make_async_copy(b.at[pl.ds(mine, 1024)], updated_out, out_sem.at[2])
    updated.start()

    for condition, copy in pending:
        @pl.when(condition)
        def _():
            copy.wait_send()

    @pl.when(is_first)
    def _():
        for block in range(4):
            direct(block).wait_send()
            for way in range(2):
                aside(block, way).wait_send()

    @pl.when(is_detour)
    def _():
        for block in range(4):
            forward(block, 0).wait_send()

    @pl.when(is_second)
    def _():
        for block in range(4):
            swap(block)[1].wait_send()

    solved0.wait()
    solved1.wait()
    updated.wait()


def body(factor, inverses, rhs):
    dma = pltpu.SemaphoreType.DMA
    return pl.pallas_call(
        kernel,
        out_shape=(jax.ShapeDtypeStruct((2, 1024, LANES), F32), jax.ShapeDtypeStruct((1024, LANES), F32)),
        in_specs=[pl.BlockSpec(memory_space=pltpu.HBM)] * 3,
        out_specs=(pl.BlockSpec(memory_space=pl.ANY), pl.BlockSpec(memory_space=pl.ANY)),
        scratch_shapes=[
            pltpu.VMEM((2048, 2048), BF16),
            pltpu.VMEM((2048, 2048), BF16),
            pltpu.VMEM((1024, 4096), BF16),
            pltpu.VMEM((4, 256, 1024), F32),
            pltpu.VMEM((4, 256, 2048), F32),
            pltpu.VMEM((2048, LANES), F32),
            pltpu.VMEM((1024, LANES), F32),
            pltpu.VMEM((1024, LANES), F32),
            pltpu.VMEM((2048, 2 * LANES), BF16),
            pltpu.VMEM((2048, 2 * LANES), BF16),
            pltpu.VMEM((4096, 2 * LANES), BF16),
            pltpu.VMEM((2048, LANES), F32),
            pltpu.VMEM((2048, LANES), F32),
            pltpu.VMEM((256, LANES), F32),
            dma((8,)), dma, dma((2, 2, SIDE)), dma((2, 2, SIDE)), dma((2, 2, SIDE)), dma((2, 2, SIDE)),
            dma((12,)), dma((4,)), dma((4,)), dma((4, 2)), dma((4,)), dma((4,)), dma((4,)), dma((3,)),
        ],
        compiler_params=pltpu.CompilerParams(collective_id=0, has_side_effects=True, vmem_limit_bytes=48 * MIB),
        cost_estimate=pl.CostEstimate(flops=2 * 2 * 2048 * 1024 * 128, bytes_accessed=18 * MIB, transcendentals=0),
        name="block_steps",
    )(factor, inverses, rhs)


def solution(mesh):
    in_specs = (P(None, "row", "col"), P(None, "col", None), P("row", "rhs"))
    out_specs = (P(None, "col", "rhs"), P(("row", "col"), "rhs"))
    return jax.shard_map(body, mesh=mesh, in_specs=in_specs, out_specs=out_specs, check_vma=False)
```

```python
import functools

import jax
import jax.numpy as jnp
from jax import lax
from jax.experimental import pallas as pl
from jax.experimental.pallas import tpu as pltpu
from jax.sharding import PartitionSpec as P

MESH = pl.DeviceIdType.MESH
F32 = jnp.float32
BF16 = jnp.bfloat16
SIDE = 8
FAR_FIRST = (4, 3, 5, 2, 6, 1, 7)
HALF = 512
CHUNK = 256
LANES = 128
MIB = 1 << 20


def split(value):
    high = value.astype(BF16)
    return high, (value - high.astype(F32)).astype(BF16)


def kernel(
    factor, inverses, rhs, solved_out, updated_out,
    first_low, second_low, inverse_low, stage, stage_wide, b, x0, x1, w0, w1, wide, acc, other, detour,
    stage_sem, b_sem, piece_sem, scatter_sem, along_sem, across_sem, direct_sem, direct_send,
    detour_sem, detour_send, forward_send, swap_sem, swap_send, out_sem, last_sem,
):
    row = lax.axis_index("row")
    col = lax.axis_index("col")
    y = lax.rem(row, SIDE)
    z = lax.div(row, SIDE)
    sibling = {"col": 1 - col}
    is_first = row == 0
    is_second = row == 1
    is_detour = (row == SIDE) | (row == 7 * SIDE)
    pending = []

    def at(yy, zz):
        return {"row": zz * SIDE + yy}

    barrier = pltpu.get_barrier_semaphore()
    for k in FAR_FIRST:
        pl.semaphore_signal(barrier, inc=1, device_id=at(lax.rem(y + k, SIDE), z), device_id_type=MESH)
        pl.semaphore_signal(barrier, inc=1, device_id=at(y, lax.rem(z + k, SIDE)), device_id_type=MESH)
    pl.semaphore_signal(barrier, inc=1, device_id=sibling, device_id_type=MESH)

    @pl.when(is_second)
    def _():
        for k in (1, 7):
            pl.semaphore_signal(barrier, inc=1, device_id={"row": k * SIDE}, device_id_type=MESH)

    def load_factor(block):
        slot = lax.rem(block, 4)
        rows = pl.ds(pl.multiple_of(lax.rem(block, 8) * 256, 256), 256)
        return pltpu.make_async_copy(factor.at[lax.div(block, 8), rows], stage.at[slot], stage_sem.at[slot])

    def load_inverse(index, block):
        rows = pl.ds(pl.multiple_of(block * 256, 256), 256)
        return pltpu.make_async_copy(inverses.at[index, rows], stage_wide.at[block], stage_sem.at[4 + block])

    def split_rows(source, slot, rows, step_rows, target, base):
        chunks = source.shape[2] // CHUNK

        def part(k, _):
            at = pl.multiple_of(k * step_rows, step_rows)
            to = pl.ds(pl.multiple_of(base + at, step_rows), step_rows)
            for q in range(chunks):
                high, low = split(source[slot, pl.ds(at, step_rows), q * CHUNK:(q + 1) * CHUNK])
                target[to, 2 * q * CHUNK:(2 * q + 1) * CHUNK] = high
                target[to, (2 * q + 1) * CHUNK:(2 * q + 2) * CHUNK] = low
            return 0

        lax.fori_loop(0, rows // step_rows, part, 0)

    def split_factor(index, target, blocks):
        def step(k, _):
            block = index * 8 + k
            load_factor(block).wait()
            split_rows(stage, lax.rem(block, 4), 256, 64, target, k * 256)

            @pl.when(block + 4 < blocks)
            def _():
                load_factor(block + 4).start()
            return 0
        lax.fori_loop(0, 8, step, 0)

    def split_inverse(index):
        def step(block, _):
            load_inverse(index, block).wait()
            split_rows(stage_wide, block, 256, 32, inverse_low, block * 256)
            return 0
        lax.fori_loop(0, 4, step, 0)

    def spread(value, target, at):
        rows = value.shape[0]
        high, low = split(value)
        chunk, inside = lax.div(at, CHUNK), lax.rem(at, CHUNK)
        for part in range(2):
            to = pl.ds(pl.multiple_of(chunk * 2 * CHUNK + part * CHUNK + inside, 64), rows)
            target[to, :LANES] = high
            target[to, LANES:] = low

    def spread_rows(source, target, begin, count):
        def step(k, _):
            at = pl.multiple_of(begin + k * CHUNK, CHUNK)
            spread(source[pl.ds(at, CHUNK), :], target, at)
            return 0
        lax.fori_loop(0, count // CHUNK, step, 0)

    def product(matrix, at, rows, weights, first, count):
        columns = slice(2 * first * CHUNK, 2 * (first + count) * CHUNK)
        both = jnp.dot(matrix[pl.ds(pl.multiple_of(at, rows), rows), columns], weights[columns, :],
                       preferred_element_type=F32)
        return both[:, :LANES] + both[:, LANES:]

    def split_product(source, slot, weights):
        total = None
        for q in range(source.shape[2] // CHUNK):
            parts = jnp.concatenate(split(source[slot, :, q * CHUNK:(q + 1) * CHUNK]), axis=0)
            term = jnp.dot(parts, weights[2 * q * CHUNK:(2 * q + 1) * CHUNK, :], preferred_element_type=F32)
            total = term if total is None else total + term
        both = total[:256, :] + total[256:, :]
        return both[:, :LANES] + both[:, LANES:]

    b_copy = pltpu.make_async_copy(rhs, b, b_sem)
    b_copy.start()

    @pl.when(is_first | is_second)
    def _():
        for block in range(4):
            load_inverse(row, jnp.int32(block)).start()

    @pl.when(jnp.logical_not(is_first))
    def _():
        for block in range(4):
            load_factor(jnp.int32(block)).start()

    def pass_barrier():
        @pl.when(is_detour)
        def _():
            pl.semaphore_wait(barrier, 16)

        @pl.when(jnp.logical_not(is_detour))
        def _():
            pl.semaphore_wait(barrier, 15)

    def layout(which, half):
        if which == 0 and half == 0:
            return 80, 32, 0, (0, 1)
        return 72, 8, (which if half == 0 else 0), ((which,) if half == 0 else (0,))

    def hub_rows(which, half, index):
        rows, _, owner, outside = layout(which, half)
        rank = index - len(outside) if owner == 0 else index - jnp.where(index > owner, 1, 0)
        return pl.ds(pl.multiple_of(half * HALF + rank * rows, 8), rows)

    def rest_rows(which, half):
        rest = layout(which, half)[1]
        return pl.ds((half + 1) * HALF - rest, rest)

    def is_hub(which, half, index):
        return functools.reduce(jnp.logical_and, [index != q for q in layout(which, half)[3]])

    def send(condition, buffer, rows, target, send_sem, recv_sem):
        copy = pltpu.make_async_remote_copy(
            src_ref=buffer.at[rows], dst_ref=buffer.at[rows], send_sem=send_sem, recv_sem=recv_sem,
            device_id=target, device_id_type=MESH,
        )

        @pl.when(condition)
        def _():
            copy.start()

        pending.append((condition, copy))

    def scatter(which, buffer, half, index):
        owner = which
        if index in layout(which, half)[3]:
            return
        place = index if half == 0 else index * SIDE + owner
        send(row == owner, buffer, hub_rows(which, half, jnp.int32(index)), {"row": place},
             scatter_sem.at[which, half, index], piece_sem.at[which, half, index])

    def among(place, holds):
        return functools.reduce(jnp.logical_or, [place == q for q in holds])

    def arrive(which, buffer, half, index, holds):
        outside = among(row, holds)

        def wait(rows):
            part = buffer.at[rows]
            pltpu.make_async_copy(part, part, piece_sem.at[which, half, index]).wait()

        @pl.when(jnp.logical_not(outside) & is_hub(which, half, index))
        def _():
            wait(hub_rows(which, half, index))

        @pl.when(jnp.logical_not(outside) & (index == layout(which, half)[2]))
        def _():
            wait(rest_rows(which, half))

    def relay(which, buffer, holds):
        for half in range(2):
            mine, cross, cross_owner = (y, z, 0) if half == 0 else (z, y, which)
            arrive(which, buffer, half, mine, holds)
            for step, sems in ((0, along_sem), (1, across_sem)):
                for k in FAR_FIRST:
                    if step == 1 and which == 0 and k == 4:
                        continue
                    if step == 0:
                        there = lax.rem(cross + k, SIDE)
                        target = y + there * SIDE if half == 0 else z * SIDE + there
                    else:
                        there = lax.rem(mine + k, SIDE)
                        target = z * SIDE + there if half == 0 else y + there * SIDE
                    go = jnp.logical_not(among(target, holds))
                    if step == 0:
                        go = go & (cross == cross_owner)
                    send(go & is_hub(which, half, mine), buffer, hub_rows(which, half, mine), {"row": target},
                         sems.at[which, half, k], piece_sem.at[which, half, mine])
                    send(go & (mine == layout(which, half)[2]), buffer, rest_rows(which, half), {"row": target},
                         sems.at[which, half, k], piece_sem.at[which, half, mine])

    def last_hop(which, buffer, holds):
        for half in range(2):
            mine = y if half == 0 else z
            source, there = lax.rem(mine + 3, SIDE), lax.rem(mine + 7, SIDE)
            arrive(which, buffer, half, source, holds)
            target = z * SIDE + there if half == 0 else y + there * SIDE
            go = jnp.logical_not(among(target, holds))
            send(go & is_hub(which, half, source), buffer, hub_rows(which, half, source), {"row": target},
                 last_sem.at[half], piece_sem.at[which, half, source])
            send(go & (source == layout(which, half)[2]), buffer, rest_rows(which, half), {"row": target},
                 last_sem.at[half], piece_sem.at[which, half, source])

    def collect(which, buffer, half, holds):
        for k in (1, 7, 2, 6, 5, 4) if which == 0 else (1, 7, 2, 6, 3, 5, 4):
            arrive(which, buffer, half, lax.rem((y if half == 0 else z) + k, SIDE), holds)

    holds0, holds1 = (0, 1), (1,)

    def direct(block):
        return pltpu.make_async_remote_copy(
            src_ref=x0.at[pl.ds(block * 256, 128)], dst_ref=x0.at[pl.ds(block * 256, 128)],
            send_sem=direct_send.at[block], recv_sem=direct_sem.at[block], device_id={"row": 1}, device_id_type=MESH)

    def aside(block, way):
        return pltpu.make_async_remote_copy(
            src_ref=x0.at[pl.ds(block * 256 + 128 + way * 64, 64)], dst_ref=detour.at[pl.ds(block * 64, 64)],
            send_sem=detour_send.at[block, way], recv_sem=detour_sem.at[block],
            device_id={"row": (SIDE, 7 * SIDE)[way]}, device_id_type=MESH)

    def forward(block, way):
        return pltpu.make_async_remote_copy(
            src_ref=detour.at[pl.ds(block * 64, 64)], dst_ref=x0.at[pl.ds(block * 256 + 128 + way * 64, 64)],
            send_sem=forward_send.at[block], recv_sem=direct_sem.at[4 + block * 2 + way],
            device_id={"row": 1}, device_id_type=MESH)

    @pl.when(is_first)
    def _():
        b_copy.wait()
        spread_rows(b, wide, 0, 2048)
        for block in range(4):
            load_inverse(0, jnp.int32(block)).wait()
            x0[pl.ds(block * 256, 256), :] = split_product(stage_wide, block, wide)
            if block == 0:
                pass_barrier()
            direct(block).start()
            for way in range(2):
                aside(block, way).start()

    @pl.when(jnp.logical_not(is_first))
    def _():
        b_copy.wait()
        split_factor(0, first_low, jnp.where(is_second, 8, 16))
        pass_barrier()

    for index in (5, 6, 7):
        scatter(0, x0, 0, index)
    for index in (4, 3, 5, 2, 6, 1, 7):
        scatter(0, x0, 1, index)
    for index in (4, 3, 2):
        scatter(0, x0, 0, index)

    for way in range(2):
        @pl.when(row == (SIDE, 7 * SIDE)[way])
        def _():
            for block in range(4):
                part = detour.at[pl.ds(block * 64, 64)]
                pltpu.make_async_copy(part, part, detour_sem.at[block]).wait()
                forward(block, way).start()

    def swap(block):
        rows = pl.ds(pl.multiple_of(block * 512, 512), 512)
        return rows, pltpu.make_async_remote_copy(
            src_ref=acc.at[rows], dst_ref=other.at[rows], send_sem=swap_send.at[block], recv_sem=swap_sem.at[block],
            device_id=sibling, device_id_type=MESH)

    @pl.when(is_second)
    def _():
        split_inverse(1)
        for chunk in range(4):
            part = x0.at[pl.ds(chunk * 256, 128)]
            pltpu.make_async_copy(part, part, direct_sem.at[chunk]).wait()
            for way in range(2):
                part = x0.at[pl.ds(chunk * 256 + 128 + way * 64, 64)]
                pltpu.make_async_copy(part, part, direct_sem.at[4 + chunk * 2 + way]).wait()
            spread_rows(x0, w0, chunk * CHUNK, CHUNK)
            for block in range(4):
                rows, copy = swap(block)
                term = product(first_low, block * 512, 512, w0, chunk, 1)
                acc[rows, :] = term if chunk == 0 else acc[rows, :] + term
                if chunk == 3:
                    copy.start()

    @pl.when(row > 1)
    def _():
        split_factor(1, second_low, 16)

    relay(0, x0, holds0)

    @pl.when(is_second)
    def _():
        for block in range(4):
            rows, copy = swap(block)
            copy.wait_recv()
            for part in range(2):
                here = pl.ds(block * 512 + part * CHUNK, CHUNK)
                value = b[here, :] - (acc[here, :] + other[here, :])
                b[here, :] = value
                spread(value, wide, jnp.int32(block * 512 + part * CHUNK))
            for part in range(2):
                here = pl.ds(part * 512, 512)
                term = product(inverse_low, part * 512, 512, wide, 2 * block, 2)
                x1[here, :] = term if block == 0 else x1[here, :] + term

    for index in (5, 4, 6, 3, 7, 0, 2):
        scatter(1, x1, 0, index)
        scatter(1, x1, 1, (index + 7) % SIDE)
    last_hop(0, x0, holds0)
    relay(1, x1, holds1)

    collect(0, x0, 0, holds0)
    collect(0, x0, 1, holds0)
    solved0 = pltpu.make_async_copy(x0, solved_out.at[0], out_sem.at[0])
    solved0.start()

    @pl.when(row > 1)
    def _():
        spread_rows(x0, w0, 0, 1024)

        def step(block, _):
            at_row = pl.multiple_of(block * 512, 512)
            acc[pl.ds(at_row, 512), :] = product(first_low, at_row, 512, w0, 0, 4)
            return 0
        lax.fori_loop(0, 4, step, 0)

    collect(1, x1, 0, holds1)

    @pl.when(row > 1)
    def _():
        spread_rows(x1, w1, 0, 512)

        def step(block, _):
            at_row = pl.multiple_of(block * 512, 512)
            rows = pl.ds(at_row, 512)
            acc[rows, :] = acc[rows, :] + product(second_low, at_row, 512, w1, 0, 2)
            return 0
        lax.fori_loop(0, 4, step, 0)

    collect(1, x1, 1, holds1)
    solved1 = pltpu.make_async_copy(x1, solved_out.at[1], out_sem.at[1])
    solved1.start()

    mine = pl.multiple_of(col * 1024, 1024)
    theirs = pl.multiple_of((1 - col) * 1024, 1024)

    def swap_half(block):
        source = pl.ds(pl.multiple_of(theirs + block * 512, 512), 512)
        return pltpu.make_async_remote_copy(
            src_ref=acc.at[source], dst_ref=other.at[pl.ds(block * 512, 512)], send_sem=swap_send.at[block],
            recv_sem=swap_sem.at[block], device_id=sibling, device_id_type=MESH)

    @pl.when(row > 1)
    def _():
        spread_rows(x1, w1, 512, 512)
        for block in range(2):
            here = pl.ds(pl.multiple_of(theirs + block * 512, 512), 512)
            acc[here, :] = acc[here, :] + product(second_low, theirs + block * 512, 512, w1, 2, 2)
            swap_half(block).start()
        for block in range(2):
            here = pl.ds(pl.multiple_of(mine + block * 512, 512), 512)
            b[here, :] = b[here, :] - (acc[here, :] + product(second_low, mine + block * 512, 512, w1, 2, 2))
        for block in range(2):
            swap_half(block).wait_recv()
            here = pl.ds(pl.multiple_of(mine + block * 512, 512), 512)
            b[here, :] = b[here, :] - other[pl.ds(block * 512, 512), :]
        for block in range(2):
            swap_half(block).wait_send()

    updated = pltpu.make_async_copy(b.at[pl.ds(mine, 1024)], updated_out, out_sem.at[2])
    updated.start()

    for condition, copy in pending:
        @pl.when(condition)
        def _():
            copy.wait_send()

    @pl.when(is_first)
    def _():
        for block in range(4):
            direct(block).wait_send()
            for way in range(2):
                aside(block, way).wait_send()

    @pl.when(is_detour)
    def _():
        for block in range(4):
            forward(block, 0).wait_send()

    @pl.when(is_second)
    def _():
        for block in range(4):
            swap(block)[1].wait_send()

    solved0.wait()
    solved1.wait()
    updated.wait()


def body(factor, inverses, rhs):
    dma = pltpu.SemaphoreType.DMA
    return pl.pallas_call(
        kernel,
        out_shape=(jax.ShapeDtypeStruct((2, 1024, LANES), F32), jax.ShapeDtypeStruct((1024, LANES), F32)),
        in_specs=[pl.BlockSpec(memory_space=pltpu.HBM)] * 3,
        out_specs=(pl.BlockSpec(memory_space=pl.ANY), pl.BlockSpec(memory_space=pl.ANY)),
        scratch_shapes=[
            pltpu.VMEM((2048, 2048), BF16),
            pltpu.VMEM((2048, 2048), BF16),
            pltpu.VMEM((1024, 4096), BF16),
            pltpu.VMEM((4, 256, 1024), F32),
            pltpu.VMEM((4, 256, 2048), F32),
            pltpu.VMEM((2048, LANES), F32),
            pltpu.VMEM((1024, LANES), F32),
            pltpu.VMEM((1024, LANES), F32),
            pltpu.VMEM((2048, 2 * LANES), BF16),
            pltpu.VMEM((2048, 2 * LANES), BF16),
            pltpu.VMEM((4096, 2 * LANES), BF16),
            pltpu.VMEM((2048, LANES), F32),
            pltpu.VMEM((2048, LANES), F32),
            pltpu.VMEM((256, LANES), F32),
            dma((8,)), dma, dma((2, 2, SIDE)), dma((2, 2, SIDE)), dma((2, 2, SIDE)), dma((2, 2, SIDE)),
            dma((12,)), dma((4,)), dma((4,)), dma((4, 2)), dma((4,)), dma((4,)), dma((4,)), dma((3,)), dma((2,)),
        ],
        compiler_params=pltpu.CompilerParams(collective_id=0, has_side_effects=True, vmem_limit_bytes=52 * MIB),
        cost_estimate=pl.CostEstimate(flops=2 * 2 * 2048 * 1024 * 128, bytes_accessed=18 * MIB, transcendentals=0),
        name="block_steps",
    )(factor, inverses, rhs)


def solution(mesh):
    in_specs = (P(None, "row", "col"), P(None, "col", None), P("row", "rhs"))
    out_specs = (P(None, "col", "rhs"), P(("row", "col"), "rhs"))
    return jax.shard_map(body, mesh=mesh, in_specs=in_specs, out_specs=out_specs, check_vma=False)
```

```python
import functools

import jax
import jax.numpy as jnp
from jax import lax
from jax.experimental import pallas as pl
from jax.experimental.pallas import tpu as pltpu
from jax.sharding import PartitionSpec as P

MESH = pl.DeviceIdType.MESH
F32 = jnp.float32
BF16 = jnp.bfloat16
SIDE = 8
FAR_FIRST = (4, 3, 5, 2, 6, 1, 7)
HALF = 512
CHUNK = 256
LANES = 128
MIB = 1 << 20


def split(value):
    high = value.astype(BF16)
    return high, (value - high.astype(F32)).astype(BF16)


def kernel(
    factor, inverses, rhs, solved_out, updated_out,
    first_low, second_low, inverse_low, stage, stage_wide, b, x0, x1, w0, w1, wide, acc, other, detour,
    stage_sem, b_sem, piece_sem, scatter_sem, along_sem, across_sem, direct_sem, direct_send,
    detour_sem, detour_send, forward_send, swap_sem, swap_send, out_sem, last_sem,
):
    row = lax.axis_index("row")
    col = lax.axis_index("col")
    y = lax.rem(row, SIDE)
    z = lax.div(row, SIDE)
    sibling = {"col": 1 - col}
    is_first = row == 0
    is_second = row == 1
    is_detour = (row == SIDE) | (row == 7 * SIDE)
    pending = []

    def at(yy, zz):
        return {"row": zz * SIDE + yy}

    barrier = pltpu.get_barrier_semaphore()
    for k in FAR_FIRST:
        pl.semaphore_signal(barrier, inc=1, device_id=at(lax.rem(y + k, SIDE), z), device_id_type=MESH)
        pl.semaphore_signal(barrier, inc=1, device_id=at(y, lax.rem(z + k, SIDE)), device_id_type=MESH)
    pl.semaphore_signal(barrier, inc=1, device_id=sibling, device_id_type=MESH)

    @pl.when(is_second)
    def _():
        for k in (1, 7):
            pl.semaphore_signal(barrier, inc=1, device_id={"row": k * SIDE}, device_id_type=MESH)

    def load_factor(block):
        slot = lax.rem(block, 4)
        rows = pl.ds(pl.multiple_of(lax.rem(block, 8) * 256, 256), 256)
        return pltpu.make_async_copy(factor.at[lax.div(block, 8), rows], stage.at[slot], stage_sem.at[slot])

    def load_inverse(index, block):
        rows = pl.ds(pl.multiple_of(block * 256, 256), 256)
        return pltpu.make_async_copy(inverses.at[index, rows], stage_wide.at[block], stage_sem.at[4 + block])

    def split_rows(source, slot, rows, step_rows, target, base):
        chunks = source.shape[2] // CHUNK

        def part(k, _):
            at = pl.multiple_of(k * step_rows, step_rows)
            to = pl.ds(pl.multiple_of(base + at, step_rows), step_rows)
            for q in range(chunks):
                high, low = split(source[slot, pl.ds(at, step_rows), q * CHUNK:(q + 1) * CHUNK])
                target[to, 2 * q * CHUNK:(2 * q + 1) * CHUNK] = high
                target[to, (2 * q + 1) * CHUNK:(2 * q + 2) * CHUNK] = low
            return 0

        lax.fori_loop(0, rows // step_rows, part, 0)

    def split_factor(index, target, blocks):
        def step(k, _):
            block = index * 8 + k
            load_factor(block).wait()
            split_rows(stage, lax.rem(block, 4), 256, 64, target, k * 256)

            @pl.when(block + 4 < blocks)
            def _():
                load_factor(block + 4).start()
            return 0
        lax.fori_loop(0, 8, step, 0)

    def split_inverse(index):
        def step(block, _):
            load_inverse(index, block).wait()
            split_rows(stage_wide, block, 256, 32, inverse_low, block * 256)
            return 0
        lax.fori_loop(0, 4, step, 0)

    def spread(value, target, at):
        rows = value.shape[0]
        high, low = split(value)
        chunk, inside = lax.div(at, CHUNK), lax.rem(at, CHUNK)
        for part in range(2):
            to = pl.ds(pl.multiple_of(chunk * 2 * CHUNK + part * CHUNK + inside, 64), rows)
            target[to, :LANES] = high
            target[to, LANES:] = low

    def spread_rows(source, target, begin, count):
        def step(k, _):
            at = pl.multiple_of(begin + k * CHUNK, CHUNK)
            spread(source[pl.ds(at, CHUNK), :], target, at)
            return 0
        lax.fori_loop(0, count // CHUNK, step, 0)

    def product(matrix, at, rows, weights, first, count):
        columns = slice(2 * first * CHUNK, 2 * (first + count) * CHUNK)
        both = jnp.dot(matrix[pl.ds(pl.multiple_of(at, rows), rows), columns], weights[columns, :],
                       preferred_element_type=F32)
        return both[:, :LANES] + both[:, LANES:]

    def split_product(source, slot, weights):
        total = None
        for q in range(source.shape[2] // CHUNK):
            parts = jnp.concatenate(split(source[slot, :, q * CHUNK:(q + 1) * CHUNK]), axis=0)
            term = jnp.dot(parts, weights[2 * q * CHUNK:(2 * q + 1) * CHUNK, :], preferred_element_type=F32)
            total = term if total is None else total + term
        both = total[:256, :] + total[256:, :]
        return both[:, :LANES] + both[:, LANES:]

    b_copy = pltpu.make_async_copy(rhs, b, b_sem)
    b_copy.start()

    @pl.when(is_first | is_second)
    def _():
        for block in range(4):
            load_inverse(row, jnp.int32(block)).start()

    @pl.when(jnp.logical_not(is_first))
    def _():
        for block in range(4):
            load_factor(jnp.int32(block)).start()

    def pass_barrier():
        @pl.when(is_detour)
        def _():
            pl.semaphore_wait(barrier, 16)

        @pl.when(jnp.logical_not(is_detour))
        def _():
            pl.semaphore_wait(barrier, 15)

    def layout(which, half):
        if which == 0 and half == 0:
            return 80, 32, 0, (0, 1)
        return 72, 8, (which if half == 0 else 0), ((which,) if half == 0 else (0,))

    def hub_rows(which, half, index):
        rows, _, owner, outside = layout(which, half)
        rank = index - len(outside) if owner == 0 else index - jnp.where(index > owner, 1, 0)
        return pl.ds(pl.multiple_of(half * HALF + rank * rows, 8), rows)

    def rest_rows(which, half):
        rest = layout(which, half)[1]
        return pl.ds((half + 1) * HALF - rest, rest)

    def is_hub(which, half, index):
        return functools.reduce(jnp.logical_and, [index != q for q in layout(which, half)[3]])

    def send(condition, buffer, rows, target, send_sem, recv_sem):
        copy = pltpu.make_async_remote_copy(
            src_ref=buffer.at[rows], dst_ref=buffer.at[rows], send_sem=send_sem, recv_sem=recv_sem,
            device_id=target, device_id_type=MESH,
        )

        @pl.when(condition)
        def _():
            copy.start()

        pending.append((condition, copy))

    def scatter(which, buffer, half, index):
        owner = which
        if index in layout(which, half)[3]:
            return
        place = index if half == 0 else index * SIDE + owner
        send(row == owner, buffer, hub_rows(which, half, jnp.int32(index)), {"row": place},
             scatter_sem.at[which, half, index], piece_sem.at[which, half, index])

    def among(place, holds):
        return functools.reduce(jnp.logical_or, [place == q for q in holds])

    def arrive(which, buffer, half, index, holds):
        outside = among(row, holds)

        def wait(rows):
            part = buffer.at[rows]
            pltpu.make_async_copy(part, part, piece_sem.at[which, half, index]).wait()

        @pl.when(jnp.logical_not(outside) & is_hub(which, half, index))
        def _():
            wait(hub_rows(which, half, index))

        @pl.when(jnp.logical_not(outside) & (index == layout(which, half)[2]))
        def _():
            wait(rest_rows(which, half))

    def relay(which, buffer, holds):
        for half in range(2):
            mine, cross, cross_owner = (y, z, 0) if half == 0 else (z, y, which)
            arrive(which, buffer, half, mine, holds)
            for step, sems in ((0, along_sem), (1, across_sem)):
                for k in FAR_FIRST:
                    if step == 1 and which == 0 and k == 4:
                        continue
                    if step == 0:
                        there = lax.rem(cross + k, SIDE)
                        target = y + there * SIDE if half == 0 else z * SIDE + there
                    else:
                        there = lax.rem(mine + k, SIDE)
                        target = z * SIDE + there if half == 0 else y + there * SIDE
                    go = jnp.logical_not(among(target, holds))
                    if step == 0:
                        go = go & (cross == cross_owner)
                    send(go & is_hub(which, half, mine), buffer, hub_rows(which, half, mine), {"row": target},
                         sems.at[which, half, k], piece_sem.at[which, half, mine])
                    send(go & (mine == layout(which, half)[2]), buffer, rest_rows(which, half), {"row": target},
                         sems.at[which, half, k], piece_sem.at[which, half, mine])

    def last_hop(which, buffer, holds):
        for half in range(2):
            mine = y if half == 0 else z
            source, there = lax.rem(mine + 3, SIDE), lax.rem(mine + 7, SIDE)
            arrive(which, buffer, half, source, holds)
            target = z * SIDE + there if half == 0 else y + there * SIDE
            go = jnp.logical_not(among(target, holds))
            send(go & is_hub(which, half, source), buffer, hub_rows(which, half, source), {"row": target},
                 last_sem.at[half], piece_sem.at[which, half, source])
            send(go & (source == layout(which, half)[2]), buffer, rest_rows(which, half), {"row": target},
                 last_sem.at[half], piece_sem.at[which, half, source])

    def collect(which, buffer, half, holds):
        for k in (1, 7, 2, 6, 5, 4) if which == 0 else (1, 7, 2, 6, 3, 5, 4):
            arrive(which, buffer, half, lax.rem((y if half == 0 else z) + k, SIDE), holds)

    holds0, holds1 = (0, 1), (1,)

    def direct(block):
        return pltpu.make_async_remote_copy(
            src_ref=x0.at[pl.ds(block * 256, 128)], dst_ref=x0.at[pl.ds(block * 256, 128)],
            send_sem=direct_send.at[block], recv_sem=direct_sem.at[block], device_id={"row": 1}, device_id_type=MESH)

    def aside(block, way):
        return pltpu.make_async_remote_copy(
            src_ref=x0.at[pl.ds(block * 256 + 128 + way * 64, 64)], dst_ref=detour.at[pl.ds(block * 64, 64)],
            send_sem=detour_send.at[block, way], recv_sem=detour_sem.at[block],
            device_id={"row": (SIDE, 7 * SIDE)[way]}, device_id_type=MESH)

    def forward(block, way):
        return pltpu.make_async_remote_copy(
            src_ref=detour.at[pl.ds(block * 64, 64)], dst_ref=x0.at[pl.ds(block * 256 + 128 + way * 64, 64)],
            send_sem=forward_send.at[block], recv_sem=direct_sem.at[4 + block * 2 + way],
            device_id={"row": 1}, device_id_type=MESH)

    @pl.when(is_first)
    def _():
        b_copy.wait()
        spread_rows(b, wide, 0, 2048)
        for block in range(4):
            load_inverse(0, jnp.int32(block)).wait()
            x0[pl.ds(block * 256, 256), :] = split_product(stage_wide, block, wide)
            if block == 0:
                pass_barrier()
            direct(block).start()
            for way in range(2):
                aside(block, way).start()

    @pl.when(jnp.logical_not(is_first))
    def _():
        b_copy.wait()
        split_factor(0, first_low, jnp.where(is_second, 8, 16))
        pass_barrier()

    for index in (5, 6, 7):
        scatter(0, x0, 0, index)
    for index in (4, 3, 5, 2, 6, 1, 7):
        scatter(0, x0, 1, index)
    for index in (4, 3, 2):
        scatter(0, x0, 0, index)

    for way in range(2):
        @pl.when(row == (SIDE, 7 * SIDE)[way])
        def _():
            for block in range(4):
                part = detour.at[pl.ds(block * 64, 64)]
                pltpu.make_async_copy(part, part, detour_sem.at[block]).wait()
                forward(block, way).start()

    def swap(block):
        rows = pl.ds(pl.multiple_of(block * 512, 512), 512)
        return rows, pltpu.make_async_remote_copy(
            src_ref=acc.at[rows], dst_ref=other.at[rows], send_sem=swap_send.at[block], recv_sem=swap_sem.at[block],
            device_id=sibling, device_id_type=MESH)

    @pl.when(is_second)
    def _():
        split_inverse(1)
        for chunk in range(4):
            part = x0.at[pl.ds(chunk * 256, 128)]
            pltpu.make_async_copy(part, part, direct_sem.at[chunk]).wait()
            for way in range(2):
                part = x0.at[pl.ds(chunk * 256 + 128 + way * 64, 64)]
                pltpu.make_async_copy(part, part, direct_sem.at[4 + chunk * 2 + way]).wait()
            spread_rows(x0, w0, chunk * CHUNK, CHUNK)
            for block in range(4):
                rows, copy = swap(block)
                term = product(first_low, block * 512, 512, w0, chunk, 1)
                acc[rows, :] = term if chunk == 0 else acc[rows, :] + term
                if chunk == 3:
                    copy.start()

    @pl.when(row > 1)
    def _():
        split_factor(1, second_low, 16)

    relay(0, x0, holds0)

    @pl.when(is_second)
    def _():
        for block in range(4):
            rows, copy = swap(block)
            copy.wait_recv()
            for part in range(2):
                here = pl.ds(block * 512 + part * CHUNK, CHUNK)
                value = b[here, :] - (acc[here, :] + other[here, :])
                b[here, :] = value
                spread(value, wide, jnp.int32(block * 512 + part * CHUNK))
            for part in range(2):
                here = pl.ds(part * 512, 512)
                term = product(inverse_low, part * 512, 512, wide, 2 * block, 2)
                x1[here, :] = term if block == 0 else x1[here, :] + term

    for index in (5, 4, 6, 3, 7, 0, 2):
        scatter(1, x1, 0, index)
        scatter(1, x1, 1, (index + 7) % SIDE)
    last_hop(0, x0, holds0)
    relay(1, x1, holds1)

    collect(0, x0, 0, holds0)
    collect(0, x0, 1, holds0)
    solved0 = pltpu.make_async_copy(x0, solved_out.at[0], out_sem.at[0])
    solved0.start()

    @pl.when(row > 1)
    def _():
        spread_rows(x0, w0, 0, 1024)

        def step(block, _):
            at_row = pl.multiple_of(block * 512, 512)
            acc[pl.ds(at_row, 512), :] = product(first_low, at_row, 512, w0, 0, 4)
            return 0
        lax.fori_loop(0, 4, step, 0)

    collect(1, x1, 0, holds1)

    @pl.when(row > 1)
    def _():
        spread_rows(x1, w1, 0, 512)

        def step(block, _):
            at_row = pl.multiple_of(block * 512, 512)
            rows = pl.ds(at_row, 512)
            acc[rows, :] = acc[rows, :] + product(second_low, at_row, 512, w1, 0, 2)
            return 0
        lax.fori_loop(0, 4, step, 0)

    collect(1, x1, 1, holds1)
    solved1 = pltpu.make_async_copy(x1, solved_out.at[1], out_sem.at[1])
    solved1.start()

    mine = pl.multiple_of(col * 1024, 1024)
    theirs = pl.multiple_of((1 - col) * 1024, 1024)

    def swap_half(block):
        source = pl.ds(pl.multiple_of(theirs + block * 512, 512), 512)
        return pltpu.make_async_remote_copy(
            src_ref=acc.at[source], dst_ref=other.at[pl.ds(block * 512, 512)], send_sem=swap_send.at[block],
            recv_sem=swap_sem.at[block], device_id=sibling, device_id_type=MESH)

    @pl.when(row > 1)
    def _():
        spread_rows(x1, w1, 512, 512)
        for block in range(2):
            here = pl.ds(pl.multiple_of(theirs + block * 512, 512), 512)
            acc[here, :] = acc[here, :] + product(second_low, theirs + block * 512, 512, w1, 2, 2)
            swap_half(block).start()
        for block in range(2):
            here = pl.ds(pl.multiple_of(mine + block * 512, 512), 512)
            b[here, :] = b[here, :] - (acc[here, :] + product(second_low, mine + block * 512, 512, w1, 2, 2))
        for block in range(2):
            swap_half(block).wait_recv()
            here = pl.ds(pl.multiple_of(mine + block * 512, 512), 512)
            b[here, :] = b[here, :] - other[pl.ds(block * 512, 512), :]
        for block in range(2):
            swap_half(block).wait_send()

    updated = pltpu.make_async_copy(b.at[pl.ds(mine, 1024)], updated_out, out_sem.at[2])
    updated.start()

    for condition, copy in pending:
        @pl.when(condition)
        def _():
            copy.wait_send()

    @pl.when(is_first)
    def _():
        for block in range(4):
            direct(block).wait_send()
            for way in range(2):
                aside(block, way).wait_send()

    @pl.when(is_detour)
    def _():
        for block in range(4):
            forward(block, 0).wait_send()

    @pl.when(is_second)
    def _():
        for block in range(4):
            swap(block)[1].wait_send()

    solved0.wait()
    solved1.wait()
    updated.wait()


def write_out(solved, updated, solved_out, updated_out, sem):
    copies = [pltpu.make_async_copy(solved.at[k], solved_out.at[k], sem.at[k]) for k in range(2)]
    copies.append(pltpu.make_async_copy(updated, updated_out, sem.at[2]))
    for copy in copies:
        copy.start()
    for copy in copies:
        copy.wait()


def body(factor, inverses, rhs):
    dma = pltpu.SemaphoreType.DMA
    results = pl.pallas_call(
        kernel,
        out_shape=(jax.ShapeDtypeStruct((2, 1024, LANES), F32), jax.ShapeDtypeStruct((1024, LANES), F32)),
        in_specs=[pl.BlockSpec(memory_space=pltpu.HBM)] * 3,
        out_specs=(pl.BlockSpec(memory_space=pl.ANY), pl.BlockSpec(memory_space=pl.ANY)),
        scratch_shapes=[
            pltpu.VMEM((2048, 2048), BF16),
            pltpu.VMEM((2048, 2048), BF16),
            pltpu.VMEM((1024, 4096), BF16),
            pltpu.VMEM((4, 256, 1024), F32),
            pltpu.VMEM((4, 256, 2048), F32),
            pltpu.VMEM((2048, LANES), F32),
            pltpu.VMEM((1024, LANES), F32),
            pltpu.VMEM((1024, LANES), F32),
            pltpu.VMEM((2048, 2 * LANES), BF16),
            pltpu.VMEM((2048, 2 * LANES), BF16),
            pltpu.VMEM((4096, 2 * LANES), BF16),
            pltpu.VMEM((2048, LANES), F32),
            pltpu.VMEM((2048, LANES), F32),
            pltpu.VMEM((256, LANES), F32),
            dma((8,)), dma, dma((2, 2, SIDE)), dma((2, 2, SIDE)), dma((2, 2, SIDE)), dma((2, 2, SIDE)),
            dma((12,)), dma((4,)), dma((4,)), dma((4, 2)), dma((4,)), dma((4,)), dma((4,)), dma((3,)), dma((2,)),
        ],
        compiler_params=pltpu.CompilerParams(collective_id=0, has_side_effects=True, vmem_limit_bytes=52 * MIB),
        cost_estimate=pl.CostEstimate(flops=2 * 2 * 2048 * 1024 * 128, bytes_accessed=18 * MIB, transcendentals=0),
        name="block_steps",
    )(factor, inverses, rhs)
    return pl.pallas_call(
        write_out,
        out_shape=tuple(jax.ShapeDtypeStruct(r.shape, r.dtype) for r in results),
        in_specs=[pl.BlockSpec(memory_space=pl.ANY)] * 2,
        out_specs=(pl.BlockSpec(memory_space=pl.ANY), pl.BlockSpec(memory_space=pl.ANY)),
        scratch_shapes=[dma((3,))],
        compiler_params=pltpu.CompilerParams(vmem_limit_bytes=MIB),
        cost_estimate=pl.CostEstimate(flops=0, bytes_accessed=3 * MIB, transcendentals=0),
        name="write_out",
    )(*results)


def solution(mesh):
    in_specs = (P(None, "row", "col"), P(None, "col", None), P("row", "rhs"))
    out_specs = (P(None, "col", "rhs"), P(("row", "col"), "rhs"))
    return jax.shard_map(body, mesh=mesh, in_specs=in_specs, out_specs=out_specs, check_vma=False)
```

```python
import functools

import jax
import jax.numpy as jnp
from jax import lax
from jax.experimental import pallas as pl
from jax.experimental.pallas import tpu as pltpu
from jax.sharding import PartitionSpec as P

MESH = pl.DeviceIdType.MESH
F32 = jnp.float32
BF16 = jnp.bfloat16
SIDE = 8
FAR_FIRST = (4, 3, 5, 2, 6, 1, 7)
HALF = 512
CHUNK = 256
LANES = 128
MIB = 1 << 20


def split(value):
    high = value.astype(BF16)
    return high, (value - high.astype(F32)).astype(BF16)


def kernel(
    factor, inverses, rhs, solved_out, updated_out,
    first_low, second_low, inverse_low, stage, stage_wide, b, x0, x1, w0, w1, wide, acc, other, detour,
    stage_sem, b_sem, piece_sem, scatter_sem, along_sem, across_sem, direct_sem, direct_send,
    detour_sem, detour_send, forward_send, swap_sem, swap_send, out_sem, last_sem, ready_sem,
):
    row = lax.axis_index("row")
    col = lax.axis_index("col")
    y = lax.rem(row, SIDE)
    z = lax.div(row, SIDE)
    sibling = {"col": 1 - col}
    is_first = row == 0
    is_second = row == 1
    is_detour = (row == SIDE) | (row == 7 * SIDE)
    pending = []

    def at(yy, zz):
        return {"row": zz * SIDE + yy}

    barrier = pltpu.get_barrier_semaphore()

    def greet(target):
        @pl.when((target["row"] != 0) | is_second | is_detour)
        def _():
            pl.semaphore_signal(barrier, inc=1, device_id=target, device_id_type=MESH)

    for k in FAR_FIRST:
        greet(at(lax.rem(y + k, SIDE), z))
        greet(at(y, lax.rem(z + k, SIDE)))

    @pl.when(jnp.logical_not(is_first))
    def _():
        pl.semaphore_signal(barrier, inc=1, device_id=sibling, device_id_type=MESH)

    @pl.when(is_second)
    def _():
        for k in (1, 7):
            pl.semaphore_signal(barrier, inc=1, device_id={"row": k * SIDE}, device_id_type=MESH)

    def load_factor(block):
        slot = lax.rem(block, 4)
        rows = pl.ds(pl.multiple_of(lax.rem(block, 8) * 256, 256), 256)
        return pltpu.make_async_copy(factor.at[lax.div(block, 8), rows], stage.at[slot], stage_sem.at[slot])

    def load_inverse(index, block):
        rows = pl.ds(pl.multiple_of(block * 256, 256), 256)
        return pltpu.make_async_copy(inverses.at[index, rows], stage_wide.at[block], stage_sem.at[4 + block])

    def split_rows(source, slot, rows, step_rows, target, base):
        chunks = source.shape[2] // CHUNK

        def part(k, _):
            at = pl.multiple_of(k * step_rows, step_rows)
            to = pl.ds(pl.multiple_of(base + at, step_rows), step_rows)
            for q in range(chunks):
                high, low = split(source[slot, pl.ds(at, step_rows), q * CHUNK:(q + 1) * CHUNK])
                target[to, 2 * q * CHUNK:(2 * q + 1) * CHUNK] = high
                target[to, (2 * q + 1) * CHUNK:(2 * q + 2) * CHUNK] = low
            return 0

        lax.fori_loop(0, rows // step_rows, part, 0)

    def split_factor(index, target, blocks):
        def step(k, _):
            block = index * 8 + k
            load_factor(block).wait()
            split_rows(stage, lax.rem(block, 4), 256, 64, target, k * 256)

            @pl.when(block + 4 < blocks)
            def _():
                load_factor(block + 4).start()
            return 0
        lax.fori_loop(0, 8, step, 0)

    def split_inverse(index):
        def step(block, _):
            load_inverse(index, block).wait()
            split_rows(stage_wide, block, 256, 32, inverse_low, block * 256)
            return 0
        lax.fori_loop(0, 4, step, 0)

    def spread(value, target, at):
        rows = value.shape[0]
        high, low = split(value)
        chunk, inside = lax.div(at, CHUNK), lax.rem(at, CHUNK)
        for part in range(2):
            to = pl.ds(pl.multiple_of(chunk * 2 * CHUNK + part * CHUNK + inside, 64), rows)
            target[to, :LANES] = high
            target[to, LANES:] = low

    def spread_rows(source, target, begin, count):
        def step(k, _):
            at = pl.multiple_of(begin + k * CHUNK, CHUNK)
            spread(source[pl.ds(at, CHUNK), :], target, at)
            return 0
        lax.fori_loop(0, count // CHUNK, step, 0)

    def product(matrix, at, rows, weights, first, count):
        columns = slice(2 * first * CHUNK, 2 * (first + count) * CHUNK)
        both = jnp.dot(matrix[pl.ds(pl.multiple_of(at, rows), rows), columns], weights[columns, :],
                       preferred_element_type=F32)
        return both[:, :LANES] + both[:, LANES:]

    def split_product(source, slot, weights):
        total = None
        for q in range(source.shape[2] // CHUNK):
            parts = jnp.concatenate(split(source[slot, :, q * CHUNK:(q + 1) * CHUNK]), axis=0)
            term = jnp.dot(parts, weights[2 * q * CHUNK:(2 * q + 1) * CHUNK, :], preferred_element_type=F32)
            total = term if total is None else total + term
        both = total[:256, :] + total[256:, :]
        return both[:, :LANES] + both[:, LANES:]

    b_copy = pltpu.make_async_copy(rhs, b, b_sem)
    b_copy.start()

    @pl.when(is_first | is_second)
    def _():
        for block in range(4):
            load_inverse(row, jnp.int32(block)).start()

    @pl.when(jnp.logical_not(is_first))
    def _():
        for block in range(4):
            load_factor(jnp.int32(block)).start()

    def pass_barrier():
        @pl.when(is_detour)
        def _():
            pl.semaphore_wait(barrier, 16)

        @pl.when(jnp.logical_not(is_detour | is_first))
        def _():
            pl.semaphore_wait(barrier, 15)

        @pl.when(jnp.logical_not(is_detour | is_second) & ((y == 0) != (z == 0)))
        def _():
            pl.semaphore_signal(ready_sem, inc=1, device_id={"row": 0}, device_id_type=MESH)

    def layout(which, half):
        if which == 0 and half == 0:
            return 80, 32, 0, (0, 1)
        return 72, 8, (which if half == 0 else 0), ((which,) if half == 0 else (0,))

    def hub_rows(which, half, index):
        rows, _, owner, outside = layout(which, half)
        rank = index - len(outside) if owner == 0 else index - jnp.where(index > owner, 1, 0)
        return pl.ds(pl.multiple_of(half * HALF + rank * rows, 8), rows)

    def rest_rows(which, half):
        rest = layout(which, half)[1]
        return pl.ds((half + 1) * HALF - rest, rest)

    def is_hub(which, half, index):
        return functools.reduce(jnp.logical_and, [index != q for q in layout(which, half)[3]])

    def send(condition, buffer, rows, target, send_sem, recv_sem):
        copy = pltpu.make_async_remote_copy(
            src_ref=buffer.at[rows], dst_ref=buffer.at[rows], send_sem=send_sem, recv_sem=recv_sem,
            device_id=target, device_id_type=MESH,
        )

        @pl.when(condition)
        def _():
            copy.start()

        pending.append((condition, copy))

    def scatter(which, buffer, half, index):
        owner = which
        if index in layout(which, half)[3]:
            return
        place = index if half == 0 else index * SIDE + owner
        send(row == owner, buffer, hub_rows(which, half, jnp.int32(index)), {"row": place},
             scatter_sem.at[which, half, index], piece_sem.at[which, half, index])

    def among(place, holds):
        return functools.reduce(jnp.logical_or, [place == q for q in holds])

    def arrive(which, buffer, half, index, holds):
        outside = among(row, holds)

        def wait(rows):
            part = buffer.at[rows]
            pltpu.make_async_copy(part, part, piece_sem.at[which, half, index]).wait()

        @pl.when(jnp.logical_not(outside) & is_hub(which, half, index))
        def _():
            wait(hub_rows(which, half, index))

        @pl.when(jnp.logical_not(outside) & (index == layout(which, half)[2]))
        def _():
            wait(rest_rows(which, half))

    def relay(which, buffer, holds):
        for half in range(2):
            mine, cross, cross_owner = (y, z, 0) if half == 0 else (z, y, which)
            arrive(which, buffer, half, mine, holds)
            for step, sems in ((0, along_sem), (1, across_sem)):
                for k in FAR_FIRST:
                    if step == 1 and which == 0 and k == 4:
                        continue
                    if step == 0:
                        there = lax.rem(cross + k, SIDE)
                        target = y + there * SIDE if half == 0 else z * SIDE + there
                    else:
                        there = lax.rem(mine + k, SIDE)
                        target = z * SIDE + there if half == 0 else y + there * SIDE
                    go = jnp.logical_not(among(target, holds))
                    if step == 0:
                        go = go & (cross == cross_owner)
                    send(go & is_hub(which, half, mine), buffer, hub_rows(which, half, mine), {"row": target},
                         sems.at[which, half, k], piece_sem.at[which, half, mine])
                    send(go & (mine == layout(which, half)[2]), buffer, rest_rows(which, half), {"row": target},
                         sems.at[which, half, k], piece_sem.at[which, half, mine])

    def last_hop(which, buffer, holds):
        for half in range(2):
            mine = y if half == 0 else z
            source, there = lax.rem(mine + 3, SIDE), lax.rem(mine + 7, SIDE)
            arrive(which, buffer, half, source, holds)
            target = z * SIDE + there if half == 0 else y + there * SIDE
            go = jnp.logical_not(among(target, holds))
            send(go & is_hub(which, half, source), buffer, hub_rows(which, half, source), {"row": target},
                 last_sem.at[half], piece_sem.at[which, half, source])
            send(go & (source == layout(which, half)[2]), buffer, rest_rows(which, half), {"row": target},
                 last_sem.at[half], piece_sem.at[which, half, source])

    def collect(which, buffer, half, holds):
        for k in (1, 7, 2, 6, 5, 4) if which == 0 else (1, 7, 2, 6, 3, 5, 4):
            arrive(which, buffer, half, lax.rem((y if half == 0 else z) + k, SIDE), holds)

    holds0, holds1 = (0, 1), (1,)

    def direct(block):
        return pltpu.make_async_remote_copy(
            src_ref=x0.at[pl.ds(block * 256, 128)], dst_ref=x0.at[pl.ds(block * 256, 128)],
            send_sem=direct_send.at[block], recv_sem=direct_sem.at[block], device_id={"row": 1}, device_id_type=MESH)

    def aside(block, way):
        return pltpu.make_async_remote_copy(
            src_ref=x0.at[pl.ds(block * 256 + 128 + way * 64, 64)], dst_ref=detour.at[pl.ds(block * 64, 64)],
            send_sem=detour_send.at[block, way], recv_sem=detour_sem.at[block],
            device_id={"row": (SIDE, 7 * SIDE)[way]}, device_id_type=MESH)

    def forward(block, way):
        return pltpu.make_async_remote_copy(
            src_ref=detour.at[pl.ds(block * 64, 64)], dst_ref=x0.at[pl.ds(block * 256 + 128 + way * 64, 64)],
            send_sem=forward_send.at[block], recv_sem=direct_sem.at[4 + block * 2 + way],
            device_id={"row": 1}, device_id_type=MESH)

    @pl.when(is_first)
    def _():
        b_copy.wait()
        spread_rows(b, wide, 0, 2048)
        for block in range(4):
            load_inverse(0, jnp.int32(block)).wait()
            x0[pl.ds(block * 256, 256), :] = split_product(stage_wide, block, wide)
            if block == 0:
                pl.semaphore_wait(barrier, 3)
            direct(block).start()
            for way in range(2):
                aside(block, way).start()

    @pl.when(jnp.logical_not(is_first))
    def _():
        b_copy.wait()
        split_factor(0, first_low, jnp.where(is_second, 8, 16))
        pass_barrier()

    @pl.when(is_first)
    def _():
        pl.semaphore_wait(ready_sem, 11)

    for index in (5, 6, 7):
        scatter(0, x0, 0, index)
    for index in (4, 3, 5, 2, 6, 1, 7):
        scatter(0, x0, 1, index)
    for index in (4, 3, 2):
        scatter(0, x0, 0, index)

    for way in range(2):
        @pl.when(row == (SIDE, 7 * SIDE)[way])
        def _():
            for block in range(4):
                part = detour.at[pl.ds(block * 64, 64)]
                pltpu.make_async_copy(part, part, detour_sem.at[block]).wait()
                forward(block, way).start()

    def swap(block):
        rows = pl.ds(pl.multiple_of(block * 512, 512), 512)
        return rows, pltpu.make_async_remote_copy(
            src_ref=acc.at[rows], dst_ref=other.at[rows], send_sem=swap_send.at[block], recv_sem=swap_sem.at[block],
            device_id=sibling, device_id_type=MESH)

    @pl.when(is_second)
    def _():
        split_inverse(1)
        for chunk in range(4):
            part = x0.at[pl.ds(chunk * 256, 128)]
            pltpu.make_async_copy(part, part, direct_sem.at[chunk]).wait()
            for way in range(2):
                part = x0.at[pl.ds(chunk * 256 + 128 + way * 64, 64)]
                pltpu.make_async_copy(part, part, direct_sem.at[4 + chunk * 2 + way]).wait()
            spread_rows(x0, w0, chunk * CHUNK, CHUNK)
            for block in range(4):
                rows, copy = swap(block)
                term = product(first_low, block * 512, 512, w0, chunk, 1)
                acc[rows, :] = term if chunk == 0 else acc[rows, :] + term
                if chunk == 3:
                    copy.start()

    @pl.when(row > 1)
    def _():
        split_factor(1, second_low, 16)

    relay(0, x0, holds0)

    @pl.when(is_second)
    def _():
        for block in range(4):
            rows, copy = swap(block)
            copy.wait_recv()
            for part in range(2):
                here = pl.ds(block * 512 + part * CHUNK, CHUNK)
                value = b[here, :] - (acc[here, :] + other[here, :])
                b[here, :] = value
                spread(value, wide, jnp.int32(block * 512 + part * CHUNK))
            for part in range(2):
                here = pl.ds(part * 512, 512)
                term = product(inverse_low, part * 512, 512, wide, 2 * block, 2)
                x1[here, :] = term if block == 0 else x1[here, :] + term

    for index in (5, 4, 6, 3, 7, 0, 2):
        scatter(1, x1, 0, index)
        scatter(1, x1, 1, (index + 7) % SIDE)
    last_hop(0, x0, holds0)
    relay(1, x1, holds1)

    collect(0, x0, 0, holds0)
    collect(0, x0, 1, holds0)
    solved0 = pltpu.make_async_copy(x0, solved_out.at[0], out_sem.at[0])
    solved0.start()

    @pl.when(row > 1)
    def _():
        spread_rows(x0, w0, 0, 1024)

        def step(block, _):
            at_row = pl.multiple_of(block * 512, 512)
            acc[pl.ds(at_row, 512), :] = product(first_low, at_row, 512, w0, 0, 4)
            return 0
        lax.fori_loop(0, 4, step, 0)

    collect(1, x1, 0, holds1)

    @pl.when(row > 1)
    def _():
        spread_rows(x1, w1, 0, 512)

        def step(block, _):
            at_row = pl.multiple_of(block * 512, 512)
            rows = pl.ds(at_row, 512)
            acc[rows, :] = acc[rows, :] + product(second_low, at_row, 512, w1, 0, 2)
            return 0
        lax.fori_loop(0, 4, step, 0)

    collect(1, x1, 1, holds1)
    solved1 = pltpu.make_async_copy(x1, solved_out.at[1], out_sem.at[1])
    solved1.start()

    mine = pl.multiple_of(col * 1024, 1024)
    theirs = pl.multiple_of((1 - col) * 1024, 1024)

    def swap_half(block):
        source = pl.ds(pl.multiple_of(theirs + block * 512, 512), 512)
        return pltpu.make_async_remote_copy(
            src_ref=acc.at[source], dst_ref=other.at[pl.ds(block * 512, 512)], send_sem=swap_send.at[block],
            recv_sem=swap_sem.at[block], device_id=sibling, device_id_type=MESH)

    @pl.when(row > 1)
    def _():
        spread_rows(x1, w1, 512, 512)
        for block in range(2):
            here = pl.ds(pl.multiple_of(theirs + block * 512, 512), 512)
            acc[here, :] = acc[here, :] + product(second_low, theirs + block * 512, 512, w1, 2, 2)
            swap_half(block).start()
        for block in range(2):
            here = pl.ds(pl.multiple_of(mine + block * 512, 512), 512)
            b[here, :] = b[here, :] - (acc[here, :] + product(second_low, mine + block * 512, 512, w1, 2, 2))
        for block in range(2):
            swap_half(block).wait_recv()
            here = pl.ds(pl.multiple_of(mine + block * 512, 512), 512)
            b[here, :] = b[here, :] - other[pl.ds(block * 512, 512), :]
        for block in range(2):
            swap_half(block).wait_send()

    updated = pltpu.make_async_copy(b.at[pl.ds(mine, 1024)], updated_out, out_sem.at[2])
    updated.start()

    for condition, copy in pending:
        @pl.when(condition)
        def _():
            copy.wait_send()

    @pl.when(is_first)
    def _():
        for block in range(4):
            direct(block).wait_send()
            for way in range(2):
                aside(block, way).wait_send()

    @pl.when(is_detour)
    def _():
        for block in range(4):
            forward(block, 0).wait_send()

    @pl.when(is_second)
    def _():
        for block in range(4):
            swap(block)[1].wait_send()

    solved0.wait()
    solved1.wait()
    updated.wait()


def write_out(solved, updated, solved_out, updated_out, sem):
    copies = [pltpu.make_async_copy(solved.at[k], solved_out.at[k], sem.at[k]) for k in range(2)]
    copies.append(pltpu.make_async_copy(updated, updated_out, sem.at[2]))
    for copy in copies:
        copy.start()
    for copy in copies:
        copy.wait()


def body(factor, inverses, rhs):
    dma = pltpu.SemaphoreType.DMA
    results = pl.pallas_call(
        kernel,
        out_shape=(jax.ShapeDtypeStruct((2, 1024, LANES), F32), jax.ShapeDtypeStruct((1024, LANES), F32)),
        in_specs=[pl.BlockSpec(memory_space=pltpu.HBM)] * 3,
        out_specs=(pl.BlockSpec(memory_space=pl.ANY), pl.BlockSpec(memory_space=pl.ANY)),
        scratch_shapes=[
            pltpu.VMEM((2048, 2048), BF16),
            pltpu.VMEM((2048, 2048), BF16),
            pltpu.VMEM((1024, 4096), BF16),
            pltpu.VMEM((4, 256, 1024), F32),
            pltpu.VMEM((4, 256, 2048), F32),
            pltpu.VMEM((2048, LANES), F32),
            pltpu.VMEM((1024, LANES), F32),
            pltpu.VMEM((1024, LANES), F32),
            pltpu.VMEM((2048, 2 * LANES), BF16),
            pltpu.VMEM((2048, 2 * LANES), BF16),
            pltpu.VMEM((4096, 2 * LANES), BF16),
            pltpu.VMEM((2048, LANES), F32),
            pltpu.VMEM((2048, LANES), F32),
            pltpu.VMEM((256, LANES), F32),
            dma((8,)), dma, dma((2, 2, SIDE)), dma((2, 2, SIDE)), dma((2, 2, SIDE)), dma((2, 2, SIDE)),
            dma((12,)), dma((4,)), dma((4,)), dma((4, 2)), dma((4,)), dma((4,)), dma((4,)), dma((3,)), dma((2,)), pltpu.SemaphoreType.REGULAR,
        ],
        compiler_params=pltpu.CompilerParams(collective_id=0, has_side_effects=True, vmem_limit_bytes=52 * MIB),
        cost_estimate=pl.CostEstimate(flops=2 * 2 * 2048 * 1024 * 128, bytes_accessed=18 * MIB, transcendentals=0),
        name="block_steps",
    )(factor, inverses, rhs)
    return pl.pallas_call(
        write_out,
        out_shape=tuple(jax.ShapeDtypeStruct(r.shape, r.dtype) for r in results),
        in_specs=[pl.BlockSpec(memory_space=pl.ANY)] * 2,
        out_specs=(pl.BlockSpec(memory_space=pl.ANY), pl.BlockSpec(memory_space=pl.ANY)),
        scratch_shapes=[dma((3,))],
        compiler_params=pltpu.CompilerParams(vmem_limit_bytes=MIB),
        cost_estimate=pl.CostEstimate(flops=0, bytes_accessed=3 * MIB, transcendentals=0),
        name="write_out",
    )(*results)


def solution(mesh):
    in_specs = (P(None, "row", "col"), P(None, "col", None), P("row", "rhs"))
    out_specs = (P(None, "col", "rhs"), P(("row", "col"), "rhs"))
    return jax.shard_map(body, mesh=mesh, in_specs=in_specs, out_specs=out_specs, check_vma=False)
```

```python
import functools

import jax
import jax.numpy as jnp
from jax import lax
from jax.experimental import pallas as pl
from jax.experimental.pallas import tpu as pltpu
from jax.sharding import PartitionSpec as P

MESH = pl.DeviceIdType.MESH
F32 = jnp.float32
BF16 = jnp.bfloat16
SIDE = 8
FAR_FIRST = (4, 3, 5, 2, 6, 1, 7)
HALF = 512
CHUNK = 256
LANES = 128
MIB = 1 << 20


def split(value):
    high = value.astype(BF16)
    return high, (value - high.astype(F32)).astype(BF16)


def kernel(
    factor, inverses, rhs, solved_out, updated_out,
    first_low, second_low, inverse_low, stage, stage_wide, b, x0, x1, w0, w1, wide, acc, other, detour,
    stage_sem, b_sem, piece_sem, scatter_sem, along_sem, across_sem, direct_sem, direct_send,
    detour_sem, detour_send, forward_send, swap_sem, swap_send, out_sem, last_sem, ready_sem,
):
    row = lax.axis_index("row")
    col = lax.axis_index("col")
    y = lax.rem(row, SIDE)
    z = lax.div(row, SIDE)
    sibling = {"col": 1 - col}
    is_first = row == 0
    is_second = row == 1
    is_detour = (row == SIDE) | (row == 7 * SIDE)
    pending = []

    def at(yy, zz):
        return {"row": zz * SIDE + yy}

    b_copy = pltpu.make_async_copy(rhs, b, b_sem)

    @pl.when(is_first)
    def _():
        b_copy.start()
        for block in range(4):
            pltpu.make_async_copy(
                inverses.at[0, pl.ds(block * 256, 256)], stage_wide.at[block], stage_sem.at[4 + block]).start()

    barrier = pltpu.get_barrier_semaphore()

    def greet(target):
        @pl.when((target["row"] != 0) | is_second | is_detour)
        def _():
            pl.semaphore_signal(barrier, inc=1, device_id=target, device_id_type=MESH)

    for k in (1, 7, 4, 3, 5, 2, 6):
        greet(at(lax.rem(y + k, SIDE), z))
        greet(at(y, lax.rem(z + k, SIDE)))

    @pl.when(jnp.logical_not(is_first))
    def _():
        pl.semaphore_signal(barrier, inc=1, device_id=sibling, device_id_type=MESH)

    @pl.when(is_second)
    def _():
        for k in (1, 7):
            pl.semaphore_signal(barrier, inc=1, device_id={"row": k * SIDE}, device_id_type=MESH)

    def load_factor(block):
        slot = lax.rem(block, 4)
        rows = pl.ds(pl.multiple_of(lax.rem(block, 8) * 256, 256), 256)
        return pltpu.make_async_copy(factor.at[lax.div(block, 8), rows], stage.at[slot], stage_sem.at[slot])

    def load_inverse(index, block):
        rows = pl.ds(pl.multiple_of(block * 256, 256), 256)
        return pltpu.make_async_copy(inverses.at[index, rows], stage_wide.at[block], stage_sem.at[4 + block])

    def split_rows(source, slot, rows, step_rows, target, base):
        chunks = source.shape[2] // CHUNK

        def part(k, _):
            at = pl.multiple_of(k * step_rows, step_rows)
            to = pl.ds(pl.multiple_of(base + at, step_rows), step_rows)
            for q in range(chunks):
                high, low = split(source[slot, pl.ds(at, step_rows), q * CHUNK:(q + 1) * CHUNK])
                target[to, 2 * q * CHUNK:(2 * q + 1) * CHUNK] = high
                target[to, (2 * q + 1) * CHUNK:(2 * q + 2) * CHUNK] = low
            return 0

        lax.fori_loop(0, rows // step_rows, part, 0)

    def split_factor(index, target, blocks):
        def step(k, _):
            block = index * 8 + k
            load_factor(block).wait()
            split_rows(stage, lax.rem(block, 4), 256, 64, target, k * 256)

            @pl.when(block + 4 < blocks)
            def _():
                load_factor(block + 4).start()
            return 0
        lax.fori_loop(0, 8, step, 0)

    def split_inverse(index):
        def step(block, _):
            load_inverse(index, block).wait()
            split_rows(stage_wide, block, 256, 32, inverse_low, block * 256)
            return 0
        lax.fori_loop(0, 4, step, 0)

    def spread(value, target, at):
        rows = value.shape[0]
        high, low = split(value)
        chunk, inside = lax.div(at, CHUNK), lax.rem(at, CHUNK)
        for part in range(2):
            to = pl.ds(pl.multiple_of(chunk * 2 * CHUNK + part * CHUNK + inside, 64), rows)
            target[to, :LANES] = high
            target[to, LANES:] = low

    def spread_rows(source, target, begin, count):
        def step(k, _):
            at = pl.multiple_of(begin + k * CHUNK, CHUNK)
            spread(source[pl.ds(at, CHUNK), :], target, at)
            return 0
        lax.fori_loop(0, count // CHUNK, step, 0)

    def product(matrix, at, rows, weights, first, count):
        columns = slice(2 * first * CHUNK, 2 * (first + count) * CHUNK)
        both = jnp.dot(matrix[pl.ds(pl.multiple_of(at, rows), rows), columns], weights[columns, :],
                       preferred_element_type=F32)
        return both[:, :LANES] + both[:, LANES:]

    def split_product(source, slot, weights):
        total = None
        for q in range(source.shape[2] // CHUNK):
            parts = jnp.concatenate(split(source[slot, :, q * CHUNK:(q + 1) * CHUNK]), axis=0)
            term = jnp.dot(parts, weights[2 * q * CHUNK:(2 * q + 1) * CHUNK, :], preferred_element_type=F32)
            total = term if total is None else total + term
        both = total[:256, :] + total[256:, :]
        return both[:, :LANES] + both[:, LANES:]

    @pl.when(is_second)
    def _():
        for block in range(4):
            load_inverse(row, jnp.int32(block)).start()

    @pl.when(jnp.logical_not(is_first))
    def _():
        b_copy.start()
        for block in range(4):
            load_factor(jnp.int32(block)).start()

    def pass_barrier():
        @pl.when(is_detour)
        def _():
            pl.semaphore_wait(barrier, 16)

        @pl.when(jnp.logical_not(is_detour | is_first))
        def _():
            pl.semaphore_wait(barrier, 15)

        @pl.when(jnp.logical_not(is_detour | is_second) & ((y == 0) != (z == 0)))
        def _():
            pl.semaphore_signal(ready_sem, inc=1, device_id={"row": 0}, device_id_type=MESH)

    def layout(which, half):
        if which == 0 and half == 0:
            return 80, 32, 0, (0, 1)
        return 72, 8, (which if half == 0 else 0), ((which,) if half == 0 else (0,))

    def hub_rows(which, half, index):
        rows, _, owner, outside = layout(which, half)
        rank = index - len(outside) if owner == 0 else index - jnp.where(index > owner, 1, 0)
        return pl.ds(pl.multiple_of(half * HALF + rank * rows, 8), rows)

    def rest_rows(which, half):
        rest = layout(which, half)[1]
        return pl.ds((half + 1) * HALF - rest, rest)

    def is_hub(which, half, index):
        return functools.reduce(jnp.logical_and, [index != q for q in layout(which, half)[3]])

    def send(condition, buffer, rows, target, send_sem, recv_sem):
        copy = pltpu.make_async_remote_copy(
            src_ref=buffer.at[rows], dst_ref=buffer.at[rows], send_sem=send_sem, recv_sem=recv_sem,
            device_id=target, device_id_type=MESH,
        )

        @pl.when(condition)
        def _():
            copy.start()

        pending.append((condition, copy))

    def scatter(which, buffer, half, index):
        owner = which
        if index in layout(which, half)[3]:
            return
        place = index if half == 0 else index * SIDE + owner
        send(row == owner, buffer, hub_rows(which, half, jnp.int32(index)), {"row": place},
             scatter_sem.at[which, half, index], piece_sem.at[which, half, index])

    def among(place, holds):
        return functools.reduce(jnp.logical_or, [place == q for q in holds])

    def arrive(which, buffer, half, index, holds):
        outside = among(row, holds)

        def wait(rows):
            part = buffer.at[rows]
            pltpu.make_async_copy(part, part, piece_sem.at[which, half, index]).wait()

        @pl.when(jnp.logical_not(outside) & is_hub(which, half, index))
        def _():
            wait(hub_rows(which, half, index))

        @pl.when(jnp.logical_not(outside) & (index == layout(which, half)[2]))
        def _():
            wait(rest_rows(which, half))

    def relay(which, buffer, holds):
        for half in range(2):
            mine, cross, cross_owner = (y, z, 0) if half == 0 else (z, y, which)
            arrive(which, buffer, half, mine, holds)
            for step, sems in ((0, along_sem), (1, across_sem)):
                for k in FAR_FIRST:
                    if step == 1 and which == 0 and k == 4:
                        continue
                    if step == 0:
                        there = lax.rem(cross + k, SIDE)
                        target = y + there * SIDE if half == 0 else z * SIDE + there
                    else:
                        there = lax.rem(mine + k, SIDE)
                        target = z * SIDE + there if half == 0 else y + there * SIDE
                    go = jnp.logical_not(among(target, holds))
                    if step == 0:
                        go = go & (cross == cross_owner)
                    send(go & is_hub(which, half, mine), buffer, hub_rows(which, half, mine), {"row": target},
                         sems.at[which, half, k], piece_sem.at[which, half, mine])
                    send(go & (mine == layout(which, half)[2]), buffer, rest_rows(which, half), {"row": target},
                         sems.at[which, half, k], piece_sem.at[which, half, mine])

    def last_hop(which, buffer, holds):
        for half in range(2):
            mine = y if half == 0 else z
            source, there = lax.rem(mine + 3, SIDE), lax.rem(mine + 7, SIDE)
            arrive(which, buffer, half, source, holds)
            target = z * SIDE + there if half == 0 else y + there * SIDE
            go = jnp.logical_not(among(target, holds))
            send(go & is_hub(which, half, source), buffer, hub_rows(which, half, source), {"row": target},
                 last_sem.at[half], piece_sem.at[which, half, source])
            send(go & (source == layout(which, half)[2]), buffer, rest_rows(which, half), {"row": target},
                 last_sem.at[half], piece_sem.at[which, half, source])

    def collect(which, buffer, half, holds):
        for k in (1, 7, 2, 6, 5, 4) if which == 0 else (1, 7, 2, 6, 3, 5, 4):
            arrive(which, buffer, half, lax.rem((y if half == 0 else z) + k, SIDE), holds)

    holds0, holds1 = (0, 1), (1,)

    def direct(block):
        return pltpu.make_async_remote_copy(
            src_ref=x0.at[pl.ds(block * 256, 128)], dst_ref=x0.at[pl.ds(block * 256, 128)],
            send_sem=direct_send.at[block], recv_sem=direct_sem.at[block], device_id={"row": 1}, device_id_type=MESH)

    def aside(block, way):
        return pltpu.make_async_remote_copy(
            src_ref=x0.at[pl.ds(block * 256 + 128 + way * 64, 64)], dst_ref=detour.at[pl.ds(block * 64, 64)],
            send_sem=detour_send.at[block, way], recv_sem=detour_sem.at[block],
            device_id={"row": (SIDE, 7 * SIDE)[way]}, device_id_type=MESH)

    def forward(block, way):
        return pltpu.make_async_remote_copy(
            src_ref=detour.at[pl.ds(block * 64, 64)], dst_ref=x0.at[pl.ds(block * 256 + 128 + way * 64, 64)],
            send_sem=forward_send.at[block], recv_sem=direct_sem.at[4 + block * 2 + way],
            device_id={"row": 1}, device_id_type=MESH)

    @pl.when(is_first)
    def _():
        b_copy.wait()
        spread_rows(b, wide, 0, 2048)
        for block in range(4):
            load_inverse(0, jnp.int32(block)).wait()
            x0[pl.ds(block * 256, 256), :] = split_product(stage_wide, block, wide)
            if block == 0:
                pl.semaphore_wait(barrier, 3)
            direct(block).start()
            for way in range(2):
                aside(block, way).start()

    @pl.when(jnp.logical_not(is_first))
    def _():
        b_copy.wait()
        split_factor(0, first_low, jnp.where(is_second, 8, 16))
        pass_barrier()

    @pl.when(is_first)
    def _():
        pl.semaphore_wait(ready_sem, 11)

    for index in (5, 6, 7):
        scatter(0, x0, 0, index)
    for index in (4, 3, 5, 2, 6, 1, 7):
        scatter(0, x0, 1, index)
    for index in (4, 3, 2):
        scatter(0, x0, 0, index)

    for way in range(2):
        @pl.when(row == (SIDE, 7 * SIDE)[way])
        def _():
            for block in range(4):
                part = detour.at[pl.ds(block * 64, 64)]
                pltpu.make_async_copy(part, part, detour_sem.at[block]).wait()
                forward(block, way).start()

    def swap(block):
        rows = pl.ds(pl.multiple_of(block * 512, 512), 512)
        return rows, pltpu.make_async_remote_copy(
            src_ref=acc.at[rows], dst_ref=other.at[rows], send_sem=swap_send.at[block], recv_sem=swap_sem.at[block],
            device_id=sibling, device_id_type=MESH)

    @pl.when(is_second)
    def _():
        split_inverse(1)
        for chunk in range(4):
            part = x0.at[pl.ds(chunk * 256, 128)]
            pltpu.make_async_copy(part, part, direct_sem.at[chunk]).wait()
            for way in range(2):
                part = x0.at[pl.ds(chunk * 256 + 128 + way * 64, 64)]
                pltpu.make_async_copy(part, part, direct_sem.at[4 + chunk * 2 + way]).wait()
            spread_rows(x0, w0, chunk * CHUNK, CHUNK)
            for block in range(4):
                rows, copy = swap(block)
                term = product(first_low, block * 512, 512, w0, chunk, 1)
                acc[rows, :] = term if chunk == 0 else acc[rows, :] + term
                if chunk == 3:
                    copy.start()

    @pl.when(row > 1)
    def _():
        split_factor(1, second_low, 16)

    relay(0, x0, holds0)

    @pl.when(is_second)
    def _():
        for block in range(4):
            rows, copy = swap(block)
            copy.wait_recv()
            for part in range(2):
                here = pl.ds(block * 512 + part * CHUNK, CHUNK)
                value = b[here, :] - (acc[here, :] + other[here, :])
                b[here, :] = value
                spread(value, wide, jnp.int32(block * 512 + part * CHUNK))
            for part in range(2):
                here = pl.ds(part * 512, 512)
                term = product(inverse_low, part * 512, 512, wide, 2 * block, 2)
                x1[here, :] = term if block == 0 else x1[here, :] + term

    for index in (5, 4, 6, 3, 7, 0, 2):
        scatter(1, x1, 0, index)
        scatter(1, x1, 1, (index + 7) % SIDE)
    last_hop(0, x0, holds0)
    relay(1, x1, holds1)

    collect(0, x0, 0, holds0)
    collect(0, x0, 1, holds0)
    solved0 = pltpu.make_async_copy(x0, solved_out.at[0], out_sem.at[0])
    solved0.start()

    @pl.when(row > 1)
    def _():
        spread_rows(x0, w0, 0, 1024)

        def step(block, _):
            at_row = pl.multiple_of(block * 512, 512)
            acc[pl.ds(at_row, 512), :] = product(first_low, at_row, 512, w0, 0, 4)
            return 0
        lax.fori_loop(0, 4, step, 0)

    collect(1, x1, 0, holds1)

    @pl.when(row > 1)
    def _():
        spread_rows(x1, w1, 0, 512)

        def step(block, _):
            at_row = pl.multiple_of(block * 512, 512)
            rows = pl.ds(at_row, 512)
            acc[rows, :] = acc[rows, :] + product(second_low, at_row, 512, w1, 0, 2)
            return 0
        lax.fori_loop(0, 4, step, 0)

    collect(1, x1, 1, holds1)
    solved1 = pltpu.make_async_copy(x1, solved_out.at[1], out_sem.at[1])
    solved1.start()

    mine = pl.multiple_of(col * 1024, 1024)
    theirs = pl.multiple_of((1 - col) * 1024, 1024)

    def swap_half(block):
        source = pl.ds(pl.multiple_of(theirs + block * 512, 512), 512)
        return pltpu.make_async_remote_copy(
            src_ref=acc.at[source], dst_ref=other.at[pl.ds(block * 512, 512)], send_sem=swap_send.at[block],
            recv_sem=swap_sem.at[block], device_id=sibling, device_id_type=MESH)

    @pl.when(row > 1)
    def _():
        spread_rows(x1, w1, 512, 512)
        for block in range(2):
            here = pl.ds(pl.multiple_of(theirs + block * 512, 512), 512)
            acc[here, :] = acc[here, :] + product(second_low, theirs + block * 512, 512, w1, 2, 2)
            swap_half(block).start()
        for block in range(2):
            here = pl.ds(pl.multiple_of(mine + block * 512, 512), 512)
            b[here, :] = b[here, :] - (acc[here, :] + product(second_low, mine + block * 512, 512, w1, 2, 2))
        for block in range(2):
            swap_half(block).wait_recv()
            here = pl.ds(pl.multiple_of(mine + block * 512, 512), 512)
            b[here, :] = b[here, :] - other[pl.ds(block * 512, 512), :]
        for block in range(2):
            swap_half(block).wait_send()

    updated = pltpu.make_async_copy(b.at[pl.ds(mine, 1024)], updated_out, out_sem.at[2])
    updated.start()

    for condition, copy in pending:
        @pl.when(condition)
        def _():
            copy.wait_send()

    @pl.when(is_first)
    def _():
        for block in range(4):
            direct(block).wait_send()
            for way in range(2):
                aside(block, way).wait_send()

    @pl.when(is_detour)
    def _():
        for block in range(4):
            forward(block, 0).wait_send()

    @pl.when(is_second)
    def _():
        for block in range(4):
            swap(block)[1].wait_send()

    solved0.wait()
    solved1.wait()
    updated.wait()


def write_out(solved, updated, solved_out, updated_out, sem):
    copies = [pltpu.make_async_copy(solved.at[k], solved_out.at[k], sem.at[k]) for k in range(2)]
    copies.append(pltpu.make_async_copy(updated, updated_out, sem.at[2]))
    for copy in copies:
        copy.start()
    for copy in copies:
        copy.wait()


def body(factor, inverses, rhs):
    dma = pltpu.SemaphoreType.DMA
    results = pl.pallas_call(
        kernel,
        out_shape=(jax.ShapeDtypeStruct((2, 1024, LANES), F32), jax.ShapeDtypeStruct((1024, LANES), F32)),
        in_specs=[pl.BlockSpec(memory_space=pltpu.HBM)] * 3,
        out_specs=(pl.BlockSpec(memory_space=pl.ANY), pl.BlockSpec(memory_space=pl.ANY)),
        scratch_shapes=[
            pltpu.VMEM((2048, 2048), BF16),
            pltpu.VMEM((2048, 2048), BF16),
            pltpu.VMEM((1024, 4096), BF16),
            pltpu.VMEM((4, 256, 1024), F32),
            pltpu.VMEM((4, 256, 2048), F32),
            pltpu.VMEM((2048, LANES), F32),
            pltpu.VMEM((1024, LANES), F32),
            pltpu.VMEM((1024, LANES), F32),
            pltpu.VMEM((2048, 2 * LANES), BF16),
            pltpu.VMEM((2048, 2 * LANES), BF16),
            pltpu.VMEM((4096, 2 * LANES), BF16),
            pltpu.VMEM((2048, LANES), F32),
            pltpu.VMEM((2048, LANES), F32),
            pltpu.VMEM((256, LANES), F32),
            dma((8,)), dma, dma((2, 2, SIDE)), dma((2, 2, SIDE)), dma((2, 2, SIDE)), dma((2, 2, SIDE)),
            dma((12,)), dma((4,)), dma((4,)), dma((4, 2)), dma((4,)), dma((4,)), dma((4,)), dma((3,)), dma((2,)), pltpu.SemaphoreType.REGULAR,
        ],
        compiler_params=pltpu.CompilerParams(collective_id=0, has_side_effects=True, vmem_limit_bytes=52 * MIB),
        cost_estimate=pl.CostEstimate(flops=2 * 2 * 2048 * 1024 * 128, bytes_accessed=18 * MIB, transcendentals=0),
        name="block_steps",
    )(factor, inverses, rhs)
    return pl.pallas_call(
        write_out,
        out_shape=tuple(jax.ShapeDtypeStruct(r.shape, r.dtype) for r in results),
        in_specs=[pl.BlockSpec(memory_space=pl.ANY)] * 2,
        out_specs=(pl.BlockSpec(memory_space=pl.ANY), pl.BlockSpec(memory_space=pl.ANY)),
        scratch_shapes=[dma((3,))],
        compiler_params=pltpu.CompilerParams(vmem_limit_bytes=MIB),
        cost_estimate=pl.CostEstimate(flops=0, bytes_accessed=3 * MIB, transcendentals=0),
        name="write_out",
    )(*results)


def solution(mesh):
    in_specs = (P(None, "row", "col"), P(None, "col", None), P("row", "rhs"))
    out_specs = (P(None, "col", "rhs"), P(("row", "col"), "rhs"))
    return jax.shard_map(body, mesh=mesh, in_specs=in_specs, out_specs=out_specs, check_vma=False)
```
